512 devices in a mesh: grp: 16 (over z_lo, core), seq: 32 (over x, y, z_hi).
Axes of the slice: x: 4, y: 4, z: 16 (z_hi: 2, z_lo: 8; z = z_hi * 8 + z_lo), core: 2. Of those that a mesh axis runs over, the one named last changes fastest.
Arguments:
- latent: float32 [16, 1024, 64], P('grp', 'seq'), may hold values from -6 to 6
- step_noise: float32 [16, 2, 1024, 64], P('grp', None, 'seq'), may hold values from -6 to 6
- start_index: int32 [16], P('grp'), may hold values from 1 to 8
- mod_table: float32 [10, 6144], replicated, may hold values from -3 to 3
- in_weight: bfloat16 [64, 3072], replicated, may hold values from -0.75 to 0.75
- in_bias: float32 [3072], replicated, may hold values from -3 to 3
- base_weight: bfloat16 [3, 32, 1536, 128], P(None, 'seq'), may hold values from -0.109375 to 0.109375
- factor_store: bfloat16 [240, 4096], P('grp'), may hold values from -0.19921875 to 0.19921875
- block_order: int32 [240], replicated, may hold values from 0 to 239, each once
- out_weight: bfloat16 [2048, 64], P('seq'), may hold values from -0.5 to 0.5
Outputs:
- latent_out: float32 [16, 1024, 64], P('grp', 'seq')
- velocity_out: float32 [16, 1024, 64], P('grp', 'seq')
The draws below stay inside these ranges and needn't reach their ends.
Inputs may be any that keep to these rules, and one draw needn't show every extreme that they name: `block_order`: every logical block is held in exactly one stored row.
All inputs are finite; a program needn't handle non-finite values.
Results may differ from the reference program's by a relative error of at most 0.017.
Values may be sent and summed in bfloat16 or wider, within the bound.
A program may use at most 64 MiB of HBM per device.

```python
import jax
import jax.numpy as jnp
from jax import lax

D = 3072
C = 64
HD = 128
RANK = 64
BW = 64
TSTEPS = 10
STEPS = 2
LEN = 1024
HEADS = 16
GROUPS = 16
NBLK = 240


def touch_ends(result, rng, low, top_value):
    dims = result.shape
    place = [jax.random.randint(jax.random.fold_in(rng, axis), (), 0, dims[axis]) for axis in range(len(dims))]
    result = result.at[tuple(place)].set(low)
    longest = dims.index(max(dims))
    place[longest] = (place[longest] + 1) % dims[longest]
    return result.at[tuple(place)].set(top_value)


def block_scale(stream_key, extent, split, low, top_value):
    loudness = 1.0
    for axis_at, shards_of in split:
        heights = jax.random.uniform(jax.random.fold_in(jax.random.fold_in(stream_key, 6), axis_at), (shards_of,), jnp.float32, low / len(split), top_value / len(split))
        loudness = loudness * jnp.repeat(jnp.exp(heights), extent[axis_at] // shards_of).reshape((-1,) + (1,) * (len(extent) - 1 - axis_at))
    return loudness


def noise(rng, shape, deviation, most, shards=(), dtype=jnp.bfloat16):
    result = deviation * jax.random.normal(rng, shape, jnp.float32)
    if shards:
        result = result * block_scale(rng, shape, shards, -0.22, 0.18)
    return jnp.clip(result, -most, most).astype(dtype)


def setup_inputs(seed: int = 0) -> dict:
    seeds = jax.random.split(jax.random.key(seed), 11)
    latent = noise(seeds[0], (GROUPS, LEN, C), 1.0, 6.0, ((0, 16), (1, 32)), jnp.float32)
    step_noise = noise(seeds[1], (GROUPS, STEPS, LEN, C), 1.0, 6.0, ((0, 16), (2, 32)), jnp.float32)
    start_index = touch_ends(jax.random.randint(seeds[2], (GROUPS,), 1, TSTEPS - STEPS + 1), jax.random.fold_in(seeds[2], 1), 1, TSTEPS - STEPS).astype(jnp.int32)
    mod_table = noise(seeds[3], (TSTEPS, 2 * D), 0.5, 3.0, (), jnp.float32)
    in_weight = noise(seeds[4], (C, D), C ** -0.5, 0.75)
    in_bias = noise(seeds[5], (D,), 0.5, 3.0, (), jnp.float32)
    base_weight = noise(seeds[6], (3, 2 * HEADS, D // 2, HD), D ** -0.5, 0.109375, ((1, 32),))
    factor_store = noise(seeds[7], (NBLK, RANK * BW), 0.034, 0.19921875, ((0, 16),))
    block_order = jax.random.permutation(seeds[8], NBLK).astype(jnp.int32)
    out_weight = noise(seeds[9], (HEADS * HD, C), HD ** -0.5, 0.5, ((0, 32),))
    return dict(latent=latent, step_noise=step_noise, start_index=start_index, mod_table=mod_table, in_weight=in_weight, in_bias=in_bias, base_weight=base_weight, factor_store=factor_store, block_order=block_order, out_weight=out_weight)


def sigma_at(index):
    remaining = 1.0 - index.astype(jnp.float32) / TSTEPS
    return 3.0 * remaining / (1.0 + 2.0 * remaining)

def plan(index):
    sigma_now = sigma_at(index)
    sigma_step = sigma_at(index + 1) - sigma_now
    spread = 0.7 * jnp.sqrt(sigma_now / (1.0 - sigma_now))
    return (sigma_now, sigma_step, spread)

def modulate(hidden, shift, scaling):
    average = lax.optimization_barrier(jnp.mean(hidden, axis=-1, keepdims=True))
    centred = hidden - average
    variance = lax.optimization_barrier(jnp.mean(centred * centred, axis=-1, keepdims=True))
    return (centred * lax.rsqrt(variance + 1e-06) * (1.0 + scaling) + shift).astype(jnp.bfloat16)

def merge_factors(factor_store, block_order, base_weight):
    logical = jnp.zeros_like(factor_store).at[block_order].set(factor_store)
    stacked = logical.reshape(NBLK, RANK, BW).transpose(1, 0, 2).reshape(RANK, NBLK * BW)
    base_full = base_weight.reshape(3, HEADS, 2, D // 2, HD).transpose(0, 2, 3, 1, 4).reshape(3, D, HEADS * HD)
    span = D + HEADS * HD
    merged = []
    for member in range(3):
        lower = stacked[:, member * span:member * span + D]
        upper = stacked[:, member * span + D:(member + 1) * span]
        delta = jnp.dot(lower.T, upper, preferred_element_type=jnp.float32)
        merged.append((base_full[member].astype(jnp.float32) + delta).astype(jnp.bfloat16))
    return merged

def attend_head(trio):
    queries, key_rows, value_rows = trio
    scores = jnp.dot(queries, key_rows.T, preferred_element_type=jnp.float32) * HD ** (-0.5)
    exponent = jnp.exp(scores)
    weights = (exponent / lax.optimization_barrier(jnp.sum(exponent, axis=-1, keepdims=True))).astype(jnp.bfloat16)
    return jnp.dot(weights, value_rows, preferred_element_type=jnp.float32).astype(jnp.bfloat16)

def reference(latent, step_noise, start_index, mod_table, in_weight, in_bias, base_weight, factor_store, block_order, out_weight):
    merged = merge_factors(factor_store, block_order, base_weight)

    def one_group(operands):
        current, noises, start = operands
        velocity = jnp.zeros_like(current)
        for section in range(STEPS):
            index = start + section
            sigma_now, sigma_step, spread = plan(index)
            table_row = lax.dynamic_index_in_dim(mod_table, index, 0, keepdims=False)
            hidden = jnp.dot(current.astype(jnp.bfloat16), in_weight, preferred_element_type=jnp.float32) + in_bias
            normed = modulate(hidden, table_row[:D], table_row[D:])
            heads_of = []
            for member in range(3):
                projected = jnp.dot(normed, merged[member], preferred_element_type=jnp.float32).astype(jnp.bfloat16)
                heads_of.append(projected.reshape(LEN, HEADS, HD).transpose(1, 0, 2))
            attended = lax.map(attend_head, (heads_of[0], heads_of[1], heads_of[2]))
            attended = attended.transpose(1, 0, 2).reshape(LEN, HEADS * HD)
            velocity = jnp.dot(attended, out_weight, preferred_element_type=jnp.float32)
            current = current * (1.0 + spread * spread / (2.0 * sigma_now) * sigma_step) + velocity * (1.0 + spread * spread * (1.0 - sigma_now) / (2.0 * sigma_now)) * sigma_step + spread * jnp.sqrt(-sigma_step) * noises[section]
        return (current, velocity)
    final_latent, final_velocity = lax.map(one_group, (latent, step_noise, start_index))
    return (final_latent, final_velocity)
```

```python
import functools
import math

import jax
import jax.numpy as jnp
from jax import lax
from jax.experimental import pallas as pl
from jax.experimental.pallas import tpu as pltpu
from jax.sharding import PartitionSpec as P

D = 3072
C = 64
HD = 128
RANK = 64
BW = 64
TSTEPS = 10
STEPS = 2
MESH = pl.DeviceIdType.MESH
F32 = jnp.float32
BF16 = jnp.bfloat16
ROWS = 80
NT = (((1,), (1,)), ((), ()))


def dot(a, b, dims=(((1,), (0,)), ((), ()))):
    return lax.dot_general(a, b, dims, preferred_element_type=F32)


def exact_dot(a, b, dims=(((1,), (0,)), ((), ()))):
    return lax.dot_general(
        a, b, dims, preferred_element_type=F32, precision=lax.Precision.HIGHEST
    )


def sigma_at(index):
    remaining = 1.0 - index.astype(F32) / TSTEPS
    return 3.0 * remaining / (1.0 + 2.0 * remaining)


def plan(index):
    sigma_now = sigma_at(index)
    sigma_step = sigma_at(index + 1) - sigma_now
    spread = 0.7 * jnp.sqrt(sigma_now / (1.0 - sigma_now))
    return (sigma_now, sigma_step, spread)


def advance(state, velocity, noise, index):
    sigma_now, sigma_step, spread = plan(jnp.full(state.shape, index, jnp.int32))
    return (
        state * (1.0 + spread * spread / (2.0 * sigma_now) * sigma_step)
        + velocity * (1.0 + spread * spread * (1.0 - sigma_now) / (2.0 * sigma_now)) * sigma_step
        + spread * jnp.sqrt(-sigma_step) * noise
    )


def token_features(state, in_weight, in_bias):
    latent_in = state.astype(BF16)
    hidden = dot(latent_in, in_weight) + in_bias
    average = jnp.mean(hidden, axis=-1, keepdims=True)
    centred = hidden - average
    variance = jnp.mean(centred * centred, axis=-1, keepdims=True)
    scale = lax.rsqrt(variance + 1e-06)
    scaled = latent_in.astype(F32) * scale
    high = scale.astype(BF16).astype(F32)
    lane = lax.broadcasted_iota(jnp.int32, scaled.shape, 1)
    rest = jnp.where(
        lane == 0, high, jnp.where(lane == 1, 1.0, jnp.where(lane == 2, scale - high, 0.0))
    )
    return jnp.concatenate([scaled, rest], axis=1).astype(BF16)


def attend(queries, tokens, score_map):
    mapped = dot(queries, score_map).astype(BF16)
    exponent = jnp.exp2(dot(mapped, tokens, NT))
    weights = (exponent / jnp.sum(exponent, axis=-1, keepdims=True)).astype(BF16)
    return dot(weights, tokens).astype(BF16)


def kernel(
    groups, heads,
    start_ref, latent_ref, noise_ref, mod_hbm, win_hbm, bias_ref, base_hbm, fac_ref, order_ref, wout_ref,
    latent_out, velocity_out,
    mod, win, base, state, noise0, wout, store, perm_even, perm_odd, folded,
    own_part, part_out, part_in, rank_out, rank_in, tokens, vel_out0, vel_in0, vel_out1, vel_in1,
    load_sem, col_send, col_recv, pair_send, pair_recv, plane_send, plane_recv,
):
    g = lax.axis_index("grp")
    s = lax.axis_index("seq")
    core, zlo = g % 2, g // 2
    zcount = groups // 2
    head, half = s // 2, s % 2
    own = latent_ref.shape[1]
    both = 2 * own
    half_d = D // 2
    store_rows = fac_ref.shape[0]
    block_rows = store.shape[2]
    pairs = D // 128
    per_member = 2 * (pairs + heads)

    def column(i):
        return ((zlo + i) % zcount * 2 + core, s)

    sibling = (g + 1 - 2 * core, s)
    partner = (g, s + 1 - 2 * half)

    def plane(h):
        return (g, h * 2 + half)

    loads = [
        pltpu.make_async_copy(src, dst, load_sem.at[i])
        for i, (src, dst) in enumerate([(win_hbm, win), (mod_hbm, mod), (base_hbm, base)])
    ]
    for load in loads:
        load.start()

    barrier = pltpu.get_barrier_semaphore()

    def greet(device):
        pl.semaphore_signal(barrier, inc=1, device_id=device, device_id_type=MESH)

    def greet_column(i, carry):
        greet(column(i))
        return carry

    def greet_plane(i, carry):
        greet(plane((head + i) % heads))
        return carry

    lax.fori_loop(1, zcount, greet_column, 0)
    greet(sibling)
    greet(partner)
    lax.fori_loop(1, heads, greet_plane, 0)

    store[core, zlo] = jnp.zeros(store.shape[2:], BF16)
    lanes = pl.ds(pl.multiple_of(head * 256, 256), 256)
    store[core, zlo, :store_rows, :] = fac_ref[:, lanes]
    own_rows = pl.ds(pl.multiple_of(half * own, own), own)
    state[own_rows, :] = latent_ref[0]
    noise0[own_rows, :] = noise_ref[0, 0]
    wout_rows = pl.ds(pl.multiple_of(half * 64, 64), 64)
    wout[wout_rows, :] = wout_ref[...]

    pl.semaphore_wait(barrier, zcount - 1 + 2 + heads - 1)

    def column_copy(i):
        place = store.at[core, zlo]
        return pltpu.make_async_remote_copy(
            src_ref=place, dst_ref=place,
            send_sem=col_send.at[i], recv_sem=col_recv.at[zlo],
            device_id=column(i), device_id_type=MESH,
        )

    def column_arrival(i):
        other = (zlo + i) % zcount
        place = store.at[core, other]
        return pltpu.make_async_remote_copy(
            src_ref=place, dst_ref=place,
            send_sem=col_send.at[i], recv_sem=col_recv.at[other],
            device_id=column(i), device_id_type=MESH,
        )

    def pair_copy(i, src, dst):
        return pltpu.make_async_remote_copy(
            src_ref=src, dst_ref=dst,
            send_sem=pair_send.at[i], recv_sem=pair_recv.at[i],
            device_id=partner, device_id_type=MESH,
        )

    def start_column(i, carry):
        column_copy(i).start()
        return carry

    lax.fori_loop(1, zcount, start_column, 0)
    pair_copies = [
        pair_copy(0, state.at[own_rows], state.at[own_rows]),
        pair_copy(1, noise0.at[own_rows], noise0.at[own_rows]),
        pair_copy(2, wout.at[wout_rows], wout.at[wout_rows]),
    ]
    other_rows = pl.ds(pl.multiple_of((1 - half) * own, own), own)
    other_wout = pl.ds(pl.multiple_of((1 - half) * 64, 64), 64)
    pair_arrivals = [
        pair_copy(0, state.at[other_rows], state.at[other_rows]),
        pair_copy(1, noise0.at[other_rows], noise0.at[other_rows]),
        pair_copy(2, wout.at[other_wout], wout.at[other_wout]),
    ]
    for copy in pair_copies:
        copy.start()

    start = start_ref[0]
    loads[0].wait()
    loads[1].wait()
    in_weight = win[...].astype(F32)
    in_bias = bias_ref[...]
    weight_centred = in_weight - jnp.mean(in_weight, axis=-1, keepdims=True)
    bias_centred = in_bias - jnp.mean(in_bias, axis=-1, keepdims=True)
    extra_row = lax.broadcasted_iota(jnp.int32, (16, D), 0)
    for step in range(STEPS):
        shift = mod[pl.ds(start + step, 1), :D]
        gain = 1.0 + mod[pl.ds(start + step, 1), D:]
        folded[step, :64, :] = (weight_centred * gain).astype(BF16)
        is_bias = (extra_row == 0) | (extra_row == 2)
        extra = jnp.where(is_bias, bias_centred * gain, jnp.where(extra_row == 1, shift, 0.0))
        folded[step, 64:80, :] = extra.astype(BF16)
        folded[step, 80:, :] = jnp.zeros((48, D), BF16)

    loads[2].wait()
    half_lanes = pl.ds(pl.multiple_of(half * half_d, 128), half_d)
    part_copies = []
    for step in range(STEPS):
        left = folded[step, :, half_lanes]
        for member in range(3):
            part = dot(left, base[member, 0])
            own_part[step, :, member * HD:(member + 1) * HD] = part
            part_out[step, :, member * HD:(member + 1) * HD] = part[:ROWS].astype(BF16)
        part_copies.append(pair_copy(3 + step, part_out.at[step], part_in.at[step]))
        part_copies[-1].start()

    for copy in pair_arrivals:
        copy.wait_recv()
    in_weight_bf = win[...]
    tokens[0, head] = token_features(state[...], in_weight_bf, in_bias)

    def plane_copy(kind, src, dst, peer):
        return pltpu.make_async_remote_copy(
            src_ref=src, dst_ref=dst,
            send_sem=plane_send.at[kind, peer], recv_sem=plane_recv.at[kind, head],
            device_id=plane(peer), device_id_type=MESH,
        )

    def plane_arrival(kind, buffer, peer):
        return pltpu.make_async_remote_copy(
            src_ref=buffer.at[peer], dst_ref=buffer.at[peer],
            send_sem=plane_send.at[kind, peer], recv_sem=plane_recv.at[kind, peer],
            device_id=plane(peer), device_id_type=MESH,
        )

    def send_plane(kind, src_of, dst):
        def body(i, carry):
            peer = (head + i) % heads
            plane_copy(kind, src_of(peer), dst.at[head], peer).start()
            return carry

        lax.fori_loop(1, heads, body, 0)

    def receive_plane(kind, buffer):
        def body(i, carry):
            plane_arrival(kind, buffer, (head + heads - i) % heads).wait_recv()
            return carry

        lax.fori_loop(1, heads, body, 0)

    def finish_plane(kind, buffer):
        def body(i, carry):
            plane_arrival(kind, buffer, (head + i) % heads).wait_send()
            return carry

        lax.fori_loop(1, heads, body, 0)

    send_plane(1, lambda peer: tokens.at[0, head], tokens.at[0])

    stored = zcount * 2 * store_rows
    row = lax.broadcasted_iota(jnp.int32, (stored, 256), 0)
    col = lax.broadcasted_iota(jnp.int32, (stored, 256), 1)
    in_block = col % block_rows
    slot = col // block_rows
    shard = slot % zcount * 2 + slot // zcount
    source = jnp.where(in_block < store_rows, shard * store_rows + in_block, -1)
    place = (row == source).astype(F32).astype(BF16)
    order = jnp.broadcast_to((order_ref[...] + 1).astype(F32), (16, stored)).astype(BF16)
    order = dot(order, place)[0:1].astype(jnp.int32) - 1
    total = (pairs + heads) * 16
    line = lax.broadcasted_iota(jnp.int32, (total, 256), 0)
    entry = line & 15
    member_of = entry - 3 * ((entry * 11) >> 5)
    target = jnp.where(entry < 12, member_of * per_member + 2 * (line >> 4), -8)
    perm_even[...] = (target == order).astype(F32).astype(BF16)
    perm_odd[...] = (target + 1 == order).astype(F32).astype(BF16)

    def wait_column(i, carry):
        column_arrival(zcount - i).wait_recv()
        return carry

    lax.fori_loop(1, zcount, wait_column, 0)
    to_sibling = pltpu.make_async_remote_copy(
        src_ref=store.at[core], dst_ref=store.at[core],
        send_sem=pair_send.at[5], recv_sem=pair_recv.at[5],
        device_id=sibling, device_id_type=MESH,
    )
    to_sibling.start()
    from_sibling = pltpu.make_async_remote_copy(
        src_ref=store.at[1 - core], dst_ref=store.at[1 - core],
        send_sem=pair_send.at[5], recv_sem=pair_recv.at[5],
        device_id=sibling, device_id_type=MESH,
    )
    from_sibling.wait_recv()
    blocks = store[...].reshape(256, 256)
    even = dot(perm_even[...], blocks)
    odd = dot(perm_odd[...], blocks)
    lane = lax.broadcasted_iota(jnp.int32, (total, 128), 1)
    entry = lax.broadcasted_iota(jnp.int32, (total, 128), 0) & 15
    rank = (entry * 11) >> 5
    even = jnp.where(rank < 2, even[:, :128], even[:, 128:])
    odd = jnp.where(rank < 2, odd[:, :128], odd[:, 128:])
    first = (rank & 1) == 0
    spread = jnp.where(
        lane < 64,
        jnp.where(first, even, pltpu.roll(even, 64, 1)),
        jnp.where(first, pltpu.roll(odd, 64, 1), odd),
    ).astype(BF16)
    lower = jnp.concatenate([spread[i * 16:(i + 1) * 16] for i in range(pairs)], axis=1)
    inner = [dot(lower, folded[step], NT).astype(BF16) for step in range(STEPS)]
    for other in range(heads):
        rank_out[other, :, 0:128] = inner[0]
        rank_out[other, :, 128:256] = inner[1]
        rank_out[other, :, 256:384] = spread[(pairs + other) * 16:(pairs + other + 1) * 16]
    rank_in[head] = rank_out[head]
    send_plane(0, lambda peer: rank_out.at[peer], rank_in)
    receive_plane(0, rank_in)
    for step in range(STEPS):
        pair_copy(3 + step, part_out.at[step], part_in.at[step]).wait_recv()
    ranks = rank_in[...].reshape(heads * 16, 384)
    entry = lax.broadcasted_iota(jnp.int32, (heads * 16, HD), 0) & 15
    member_of = entry - 3 * ((entry * 11) >> 5)
    upper = ranks[:, 256:].astype(F32)
    upper = jnp.concatenate(
        [jnp.where(member_of == member, upper, 0.0) for member in range(3)], axis=1
    ).astype(BF16)
    low_rank = dot(ranks[:, :256].astype(F32).T.astype(BF16), upper)
    out_weight = wout[...].astype(F32)
    score_maps, value_maps = [], []
    for step in range(STEPS):
        received = jnp.concatenate(
            [part_in[step].astype(F32), jnp.zeros((128 - ROWS, 3 * HD), F32)], axis=0
        )
        full = own_part[step] + received + low_rank[step * 128:(step + 1) * 128]
        score_map = exact_dot(full[:, :HD], full[:, HD:2 * HD], NT)
        score_maps.append((score_map * (HD ** (-0.5) * math.log2(math.e))).astype(BF16))
        value_map = exact_dot(full[:, 2 * HD:], out_weight)
        nothing = jnp.zeros_like(value_map)
        value_maps.append(
            jnp.concatenate(
                [
                    jnp.concatenate([value_map, nothing], axis=1),
                    jnp.concatenate([nothing, value_map], axis=1),
                ],
                axis=0,
            ).astype(BF16)
        )

    owners = 4
    receive_plane(1, tokens.at[0])
    keys = tokens[0].reshape(heads * both, 128)
    for part in range(heads // owners):
        first_owner = (head // owners + part) % (heads // owners) * owners
        queries = tokens[0, pl.ds(first_owner, owners)].reshape(owners * both, 128)
        attended = attend(queries, keys, score_maps[0]).reshape(owners, both, 128)
        sides = jnp.concatenate(
            [
                attended[:, :own].reshape(owners * own, 128),
                attended[:, own:].reshape(owners * own, 128),
            ],
            axis=1,
        )
        velocity = dot(sides, value_maps[0]).astype(BF16).reshape(owners, own, 128)
        vel_out0[pl.ds(first_owner, owners)] = velocity
        for i in range(owners):
            peer = first_owner + i

            @pl.when(peer != head)
            def _():
                plane_copy(2, vel_out0.at[peer], vel_in0.at[head], peer).start()

    vel_in0[head] = vel_out0[head]
    pair_copies[0].wait_send()
    receive_plane(2, vel_in0)
    velocity = jnp.sum(vel_in0[...].astype(F32), axis=0)
    velocity = jnp.concatenate([velocity[:, :C], velocity[:, C:]], axis=0)
    state[...] = advance(state[...], velocity, noise0[...], start)
    tokens[1, head] = token_features(state[...], in_weight_bf, in_bias)
    send_plane(3, lambda peer: tokens.at[1, head], tokens.at[1])
    receive_plane(3, tokens.at[1])

    owners = 8
    keys = tokens[1].reshape(heads * both, 128)
    quarter = own // 2
    for part in range(heads // owners):
        first_owner = (head // owners + part) % (heads // owners) * owners
        queries = tokens[1, pl.ds(first_owner, owners), own_rows, :].reshape(owners * own, 128)
        attended = attend(queries, keys, score_maps[1]).reshape(owners, own, 128)
        sides = jnp.concatenate(
            [
                attended[:, :quarter].reshape(owners * quarter, 128),
                attended[:, quarter:].reshape(owners * quarter, 128),
            ],
            axis=1,
        )
        velocity = dot(sides, value_maps[1]).astype(BF16).reshape(owners, quarter, 128)
        vel_out1[pl.ds(first_owner, owners)] = velocity
        for i in range(owners):
            peer = first_owner + i

            @pl.when(peer != head)
            def _():
                plane_copy(4, vel_out1.at[peer], vel_in1.at[head], peer).start()

    vel_in1[head] = vel_out1[head]
    receive_plane(4, vel_in1)
    velocity = jnp.sum(vel_in1[...].astype(F32), axis=0)
    velocity = jnp.concatenate([velocity[:, :C], velocity[:, C:]], axis=0)
    latent_out[0] = advance(state[own_rows, :], velocity, noise_ref[0, 1], start + 1)
    velocity_out[0] = velocity

    def finish_column(i, carry):
        column_copy(i).wait_send()
        return carry

    lax.fori_loop(1, zcount, finish_column, 0)
    to_sibling.wait_send()
    for copy in pair_copies[1:] + part_copies:
        copy.wait_send()
    finish_plane(0, rank_in)
    finish_plane(1, tokens.at[0])
    finish_plane(2, vel_in0)
    finish_plane(3, tokens.at[1])
    finish_plane(4, vel_in1)


def shards(groups, heads):
    def run(
        latent, step_noise, start_index, mod_table, in_weight, in_bias,
        base_weight, factor_store, block_order, out_weight,
    ):
        own = latent.shape[1]
        block_rows = (factor_store.shape[0] + 15) // 16 * 16
        total = (D // 128 + heads) * 16
        vmem = pl.BlockSpec(memory_space=pltpu.VMEM)
        anywhere = pl.BlockSpec(memory_space=pl.ANY)
        return pl.pallas_call(
            functools.partial(kernel, groups, heads),
            out_shape=(
                jax.ShapeDtypeStruct(latent.shape, F32),
                jax.ShapeDtypeStruct(latent.shape, F32),
            ),
            in_specs=[
                pl.BlockSpec(memory_space=pltpu.SMEM),
                vmem, vmem, anywhere, anywhere, vmem, anywhere, vmem, vmem, vmem,
            ],
            out_specs=(vmem, vmem),
            scratch_shapes=[
                pltpu.VMEM(mod_table.shape, F32),
                pltpu.VMEM(in_weight.shape, BF16),
                pltpu.VMEM(base_weight.shape, BF16),
                pltpu.VMEM((2 * own, C), F32),
                pltpu.VMEM((2 * own, C), F32),
                pltpu.VMEM((HD, C), BF16),
                pltpu.VMEM((2, groups // 2, block_rows, 256), BF16),
                pltpu.VMEM((total, 256), BF16),
                pltpu.VMEM((total, 256), BF16),
                pltpu.VMEM((STEPS, 128, D), BF16),
                pltpu.VMEM((STEPS, 128, 3 * HD), F32),
                pltpu.VMEM((STEPS, ROWS, 3 * HD), BF16),
                pltpu.VMEM((STEPS, ROWS, 3 * HD), BF16),
                pltpu.VMEM((heads, 16, 384), BF16),
                pltpu.VMEM((heads, 16, 384), BF16),
                pltpu.VMEM((STEPS, heads, 2 * own, 128), BF16),
                pltpu.VMEM((heads, own, 128), BF16),
                pltpu.VMEM((heads, own, 128), BF16),
                pltpu.VMEM((heads, own // 2, 128), BF16),
                pltpu.VMEM((heads, own // 2, 128), BF16),
                pltpu.SemaphoreType.DMA((3,)),
                pltpu.SemaphoreType.DMA((max(groups // 2, 2),)),
                pltpu.SemaphoreType.DMA((max(groups // 2, 2),)),
                pltpu.SemaphoreType.DMA((6,)),
                pltpu.SemaphoreType.DMA((6,)),
                pltpu.SemaphoreType.DMA((5, heads)),
                pltpu.SemaphoreType.DMA((5, heads)),
            ],
            compiler_params=pltpu.CompilerParams(
                collective_id=0, has_side_effects=True, vmem_limit_bytes=48 * 1024 * 1024
            ),
        )(
            start_index, latent, step_noise, mod_table, in_weight, in_bias.reshape(1, -1),
            base_weight, factor_store, block_order.reshape(1, -1), out_weight,
        )

    return run


def solution(mesh):
    in_specs = (
        P("grp", "seq", None),
        P("grp", None, "seq", None),
        P("grp"),
        P(),
        P(),
        P(),
        P(None, "seq", None, None),
        P("grp", None),
        P(),
        P("seq", None),
    )
    out_specs = (P("grp", "seq", None), P("grp", "seq", None))
    run = shards(mesh.shape["grp"], mesh.shape["seq"] // 2)
    return jax.shard_map(run, mesh=mesh, in_specs=in_specs, out_specs=out_specs, check_vma=False)
```

```python
import functools
import math

import jax
import jax.numpy as jnp
from jax import lax
from jax.experimental import pallas as pl
from jax.experimental.pallas import tpu as pltpu
from jax.sharding import PartitionSpec as P

D = 3072
C = 64
HD = 128
RANK = 64
BW = 64
TSTEPS = 10
STEPS = 2
MESH = pl.DeviceIdType.MESH
F32 = jnp.float32
BF16 = jnp.bfloat16
QUERY = 64
KEY = 80
ROWS = 80
MAP_ROWS = 96
NT = (((1,), (1,)), ((), ()))
SIDE = 4
OFFSETS = (
    (2, 2), (2, 1), (2, 3), (1, 2), (3, 2), (1, 1), (3, 3), (1, 3), (3, 1),
    (2, 0), (0, 2), (1, 0), (3, 0), (0, 1), (0, 3),
)


def dot(a, b, dims=(((1,), (0,)), ((), ()))):
    return lax.dot_general(a, b, dims, preferred_element_type=F32)


def exact_dot(a, b, dims=(((1,), (0,)), ((), ()))):
    return lax.dot_general(
        a, b, dims, preferred_element_type=F32, precision=lax.Precision.HIGHEST
    )


def sigma_at(index):
    remaining = 1.0 - index.astype(F32) / TSTEPS
    return 3.0 * remaining / (1.0 + 2.0 * remaining)


def plan(index):
    sigma_now = sigma_at(index)
    sigma_step = sigma_at(index + 1) - sigma_now
    spread = 0.7 * jnp.sqrt(sigma_now / (1.0 - sigma_now))
    return (sigma_now, sigma_step, spread)


def advance(state, velocity, noise, index):
    sigma_now, sigma_step, spread = plan(jnp.full(state.shape, index, jnp.int32))
    return (
        state * (1.0 + spread * spread / (2.0 * sigma_now) * sigma_step)
        + velocity * (1.0 + spread * spread * (1.0 - sigma_now) / (2.0 * sigma_now)) * sigma_step
        + spread * jnp.sqrt(-sigma_step) * noise
    )


def token_features(state, in_weight, in_bias):
    latent_in = state.astype(BF16)
    hidden = dot(latent_in, in_weight) + in_bias
    average = jnp.mean(hidden, axis=-1, keepdims=True)
    centred = hidden - average
    variance = jnp.mean(centred * centred, axis=-1, keepdims=True)
    scale = lax.rsqrt(variance + 1e-06)
    scaled = latent_in.astype(F32) * scale
    high = scale.astype(BF16).astype(F32)
    lane = lax.broadcasted_iota(jnp.int32, scaled.shape, 1)
    entry = jnp.where(lane < 2 * (KEY - QUERY), lane & (KEY - QUERY - 1), 3)
    rest = jnp.where(
        entry == 0, high, jnp.where(entry == 1, 1.0, jnp.where(entry == 2, scale - high, 0.0))
    )
    return jnp.concatenate([scaled, rest], axis=1).astype(BF16)


def kernel(
    groups, heads,
    start_ref, latent_hbm, noise_hbm, mod_hbm, win_hbm, bias_hbm, base_hbm, fac_hbm, order_hbm, wout_hbm,
    latent_out, velocity_out,
    mod, win, bias_ref, base, fac_ref, order_ref, latent0, noise0, noise1, wout_half,
    pair_state, wout, store, perm_even, perm_odd, folded,
    own_part, part_out, part_in, rank_out, rank_in, tokens, maps_out, maps_in,
    load_sem, col_send, col_recv, pair_send, pair_recv, plane_send, plane_recv, ready,
):
    g = lax.axis_index("grp")
    s = lax.axis_index("seq")
    core, zlo = g % 2, g // 2
    zcount = groups // 2
    head, half = s // 2, s % 2
    own = latent_hbm.shape[1]
    both = 2 * own
    half_d = D // 2
    store_rows = fac_hbm.shape[0]
    block_rows = store.shape[2]
    pairs = D // 128
    per_member = 2 * (pairs + heads)

    sibling = (g + 1 - 2 * core, s)
    partner = (g, s + 1 - 2 * half)

    def column_target(j):
        return jnp.where(zlo < zcount // 2, zcount - 1 - j, j)

    def column(other):
        return (other * 2 + core, s)

    def peer_at(offset):
        dx, dy = offset
        return (head // SIDE + dx) % SIDE * SIDE + (head % SIDE + dy) % SIDE

    def plane(h):
        return (g, h * 2 + half)

    loads = {
        name: pltpu.make_async_copy(src, dst, load_sem.at[i])
        for i, (name, src, dst) in enumerate(
            [
                ("in_weight", win_hbm, win),
                ("table", mod_hbm, mod),
                ("in_bias", bias_hbm, bias_ref),
                ("base", base_hbm, base),
                ("factors", fac_hbm, fac_ref),
                ("latent", latent_hbm.at[0], latent0),
                ("noise0", noise_hbm.at[0, 0], noise0),
                ("out_weight", wout_hbm, wout_half),
                ("order", order_hbm, order_ref),
                ("noise1", noise_hbm.at[0, 1], noise1),
            ]
        )
    }
    for load in loads.values():
        load.start()

    barrier = pltpu.get_barrier_semaphore()

    def greet(device):
        pl.semaphore_signal(barrier, inc=1, device_id=device, device_id_type=MESH)

    @pl.when(half == 0)
    def _():
        greet(partner)

    for j in range(zcount):
        other = column_target(j)

        @pl.when(other != zlo)
        def _():
            greet(column(other))

    for offset in OFFSETS:
        greet(plane(peer_at(offset)))
    greet(sibling)

    arriving, leaving = {}, {}

    start = start_ref[0]
    for name in ("in_weight", "in_bias", "table"):
        loads[name].wait()
    in_weight = win[...].astype(F32)
    in_bias = bias_ref[...]
    weight_centred = in_weight - jnp.mean(in_weight, axis=-1, keepdims=True)
    bias_centred = in_bias - jnp.mean(in_bias, axis=-1, keepdims=True)
    extra_row = lax.broadcasted_iota(jnp.int32, (16, D), 0)
    for step in range(STEPS):
        shift = mod[pl.ds(start + step, 1), :D]
        gain = 1.0 + mod[pl.ds(start + step, 1), D:]
        folded[step, :64, :] = (weight_centred * gain).astype(BF16)
        is_bias = (extra_row == 0) | (extra_row == 2)
        extra = jnp.where(is_bias, bias_centred * gain, jnp.where(extra_row == 1, shift, 0.0))
        folded[step, 64:80, :] = extra.astype(BF16)
        folded[step, 80:, :] = jnp.zeros((48, D), BF16)

    loads["base"].wait()
    half_lanes = pl.ds(pl.multiple_of(half * half_d, 128), half_d)
    for member in range(3):
        part = dot(folded[:, :, half_lanes].reshape(STEPS * 128, half_d), base[member, 0])
        for step in range(STEPS):
            piece = part[step * 128:(step + 1) * 128]
            own_part[step, :, member * HD:(member + 1) * HD] = piece
            part_out[step, :, member * HD:(member + 1) * HD] = piece[:ROWS].astype(BF16)

    loads["factors"].wait()
    store[core, zlo] = jnp.zeros(store.shape[2:], BF16)
    lanes = pl.ds(pl.multiple_of(head * 256, 256), 256)
    store[core, zlo, :store_rows, :] = fac_ref[:, lanes]
    for name in ("latent", "noise0", "out_weight"):
        loads[name].wait()
    own_rows = pl.ds(pl.multiple_of(half * own, own), own)
    other_rows = pl.ds(pl.multiple_of((1 - half) * own, own), own)
    pair_state[own_rows, :] = jnp.concatenate([latent0[...], noise0[...]], axis=1)
    packed = wout_half[...].astype(F32)
    wout[half] = jnp.concatenate([packed[:32], packed[32:]], axis=1).astype(BF16)
    for step in range(STEPS):
        maps_in[step, :, MAP_ROWS:, :] = jnp.zeros((heads, 128 - MAP_ROWS, 128), BF16)

    pl.semaphore_wait(barrier, zcount - 1 + 1 + heads - 1 + half)

    def arrived(name):
        arriving.pop(name)()

    def left(name):
        leaving.pop(name)()

    def column_copy(slot, other):
        place = store.at[core, slot]
        return pltpu.make_async_remote_copy(
            src_ref=place, dst_ref=place,
            send_sem=col_send.at[other], recv_sem=col_recv.at[slot],
            device_id=column(other), device_id_type=MESH,
        )

    def each_column(action):
        for j in range(zcount):
            other = column_target(j)

            @pl.when(other != zlo)
            def _():
                action(other)

    def pair_copy(i, src, dst, device=partner):
        return pltpu.make_async_remote_copy(
            src_ref=src, dst_ref=dst,
            send_sem=pair_send.at[i], recv_sem=pair_recv.at[i],
            device_id=device, device_id_type=MESH,
        )

    def exchange(name, i, out, into, device=partner):
        copy = pair_copy(i, out, out, device)
        copy.start()
        arriving[name] = pair_copy(i, into, into, device).wait_recv
        leaving[name] = copy.wait_send

    each_column(lambda other: column_copy(zlo, other).start())
    arriving["column"] = lambda: each_column(lambda other: column_copy(other, other).wait_recv())
    leaving["column"] = lambda: each_column(lambda other: column_copy(zlo, other).wait_send())
    state_copy = pair_copy(0, pair_state.at[own_rows], pair_state.at[own_rows])
    wout_copy = pair_copy(1, wout.at[half], wout.at[half])
    part_copies = [pair_copy(3 + step, part_out.at[step], part_in.at[step]) for step in range(STEPS)]

    def start_pair():
        state_copy.start()
        part_copies[0].start()
        wout_copy.start()

    @pl.when(half == 1)
    def _():
        pl.semaphore_signal(ready, inc=1, device_id=partner, device_id_type=MESH)
        start_pair()


    def plane_copy(kind, src, dst, peer, slot):
        return pltpu.make_async_remote_copy(
            src_ref=src, dst_ref=dst,
            send_sem=plane_send.at[kind, peer], recv_sem=plane_recv.at[kind, slot],
            device_id=plane(peer), device_id_type=MESH,
        )

    def send_plane(kind, src_of, place_of):
        def receive(offsets=OFFSETS):
            for offset in offsets:
                peer = peer_at(offset)
                plane_copy(kind, src_of(peer), place_of(peer), peer, peer).wait_recv()

        def finish():
            for offset in OFFSETS:
                peer = peer_at(offset)
                plane_copy(kind, src_of(peer), place_of(head), peer, head).wait_send()

        for offset in OFFSETS:
            peer = peer_at(offset)
            plane_copy(kind, src_of(peer), place_of(head), peer, head).start()
        arriving["plane", kind] = receive
        leaving["plane", kind] = finish
        return receive

    stored = zcount * 2 * store_rows
    row = lax.broadcasted_iota(jnp.int32, (stored, 256), 0)
    col = lax.broadcasted_iota(jnp.int32, (stored, 256), 1)
    in_block = col % block_rows
    slot = col // block_rows
    shard = slot % zcount * 2 + slot // zcount
    source = jnp.where(in_block < store_rows, shard * store_rows + in_block, -1)
    place = (row == source).astype(F32).astype(BF16)
    loads["order"].wait()
    order = jnp.broadcast_to((order_ref[...] + 1).astype(F32), (16, stored)).astype(BF16)
    order = dot(order, place)[0:1].astype(jnp.int32) - 1
    total = (pairs + heads) * 16
    line = lax.broadcasted_iota(jnp.int32, (total, 256), 0)
    entry = line & 15
    member_of = entry - 3 * ((entry * 11) >> 5)
    target = jnp.where(entry < 12, member_of * per_member + 2 * (line >> 4), -8)
    perm_even[...] = (target == order).astype(F32).astype(BF16)
    perm_odd[...] = (target + 1 == order).astype(F32).astype(BF16)

    arrived("column")
    exchange("sibling", 2, store.at[core], store.at[1 - core], sibling)
    arrived("sibling")
    blocks = store[...].reshape(256, 256)
    even = dot(perm_even[...], blocks)
    odd = dot(perm_odd[...], blocks)
    lane = lax.broadcasted_iota(jnp.int32, (total, 128), 1)
    entry = lax.broadcasted_iota(jnp.int32, (total, 128), 0) & 15
    rank = (entry * 11) >> 5
    even = jnp.where(rank < 2, even[:, :128], even[:, 128:])
    odd = jnp.where(rank < 2, odd[:, :128], odd[:, 128:])
    first = (rank & 1) == 0
    spread = jnp.where(
        lane < 64,
        jnp.where(first, even, pltpu.roll(even, 64, 1)),
        jnp.where(first, pltpu.roll(odd, 64, 1), odd),
    ).astype(BF16)
    lower = jnp.concatenate([spread[i * 16:(i + 1) * 16] for i in range(pairs)], axis=1)
    inner = [dot(lower, folded[step], NT).astype(BF16) for step in range(STEPS)]
    for other in range(heads):
        rank_out[other, :, 0:128] = inner[0]
        rank_out[other, :, 128:256] = inner[1]
        rank_out[other, :, 256:384] = spread[(pairs + other) * 16:(pairs + other + 1) * 16]
    rank_in[head] = rank_out[head]
    send_plane(0, lambda peer: rank_out.at[peer], lambda slot: rank_in.at[slot])

    @pl.when(half == 0)
    def _():
        pl.semaphore_wait(ready, 1)
        start_pair()

    part_copies[1].start()
    place = pair_state.at[other_rows]
    arriving["state"] = pair_copy(0, place, place).wait_recv
    place = wout.at[1 - half]
    arriving["out_weight"] = pair_copy(1, place, place).wait_recv
    leaving["state"] = state_copy.wait_send
    leaving["out_weight"] = wout_copy.wait_send
    for step in range(STEPS):
        arriving["part", step] = part_copies[step].wait_recv
        leaving["part", step] = part_copies[step].wait_send

    arrived("state")
    in_weight_bf = win[...]
    tokens[0, head] = token_features(pair_state[:, :C], in_weight_bf, in_bias)
    send_plane(1, lambda peer: tokens.at[0, head], lambda slot: tokens.at[0, slot])

    arrived(("plane", 0))
    ranks = rank_in[...].reshape(heads * 16, 384)
    entry = lax.broadcasted_iota(jnp.int32, (heads * 16, HD), 0) & 15
    member_of = entry - 3 * ((entry * 11) >> 5)
    upper = ranks[:, 256:].astype(F32)
    upper = jnp.concatenate(
        [jnp.where(member_of == member, upper, 0.0) for member in range(3)], axis=1
    ).astype(BF16)
    low_rank = dot(ranks[:, :256].astype(F32).T.astype(BF16), upper)
    arrived("out_weight")
    sides = [wout[i].astype(F32) for i in range(2)]
    out_weight = jnp.concatenate(
        [side[:, i * C:(i + 1) * C] for side in sides for i in range(2)], axis=0
    )
    got_maps = []

    def make_maps(step):
        arrived(("part", step))
        received = jnp.concatenate(
            [part_in[step].astype(F32), jnp.zeros((128 - ROWS, 3 * HD), F32)], axis=0
        )
        full = own_part[step] + received + low_rank[step * 128:(step + 1) * 128]
        to_score = HD ** (-0.5) * math.log2(math.e)
        queries, keys = full[:, :HD] * to_score, full[:, HD:2 * HD]
        score_map = exact_dot(queries[:ROWS], keys[:QUERY], NT)
        other_columns = exact_dot(keys[QUERY:ROWS], queries, NT)
        value_map = exact_dot(full[:ROWS, 2 * HD:], out_weight)
        maps_out[step, :ROWS, :] = jnp.concatenate([score_map, value_map], axis=1).astype(BF16)
        maps_out[step, ROWS:, :] = other_columns.astype(BF16)
        maps_in[step, head, :MAP_ROWS, :] = maps_out[step]

    def send_maps(step):
        got_maps.append(
            send_plane(
                2 + step,
                lambda peer: maps_out.at[step],
                lambda slot: maps_in.at[step, slot, pl.ds(0, MAP_ROWS)],
            )
        )

    make_maps(0)
    send_maps(0)
    make_maps(1)

    def first_lanes(features):
        lane = lax.broadcasted_iota(jnp.int32, features.shape, 1)
        return jnp.where(lane < KEY, features, jnp.zeros_like(features))

    def mapped(features, step, slots):
        features = first_lanes(features)
        lane = lax.broadcasted_iota(jnp.int32, features.shape, 1)
        result = []
        for slot in slots:
            maps = maps_in[step, slot]
            columns, others = dot(features, maps), dot(features, maps, NT)
            result.append(jnp.where(lane < QUERY, columns, jnp.where(lane < KEY, 0.0, others)))
        return jnp.concatenate(result, axis=0).astype(BF16)

    def attend(queries, keys, step, slots):
        count = queries.shape[0] // len(slots)
        exponent = jnp.exp2(dot(queries, keys, NT))
        weights = exponent * (1.0 / jnp.sum(exponent, axis=-1, keepdims=True))
        attended = first_lanes(dot(weights.astype(BF16), keys)).astype(BF16)
        sides = jnp.concatenate(
            [attended[i * count:(i + 1) * count] for i in range(len(slots))], axis=1
        )
        return dot(sides, jnp.concatenate([maps_in[step, slot] for slot in slots], axis=0))

    near_first = ((0, 0),) + OFFSETS[::-1]

    arrived(("plane", 1))
    keys = tokens[0].reshape(heads * both, 128)
    features = tokens[0, head]
    arriving.pop(("plane", 2))
    velocity = jnp.zeros((both, 128), F32)
    for i in range(0, heads, 4):
        offsets = near_first[i:i + 4]
        got_maps[0](offsets[1:] if i == 0 else offsets)
        slots = [peer_at(offset) for offset in offsets]
        if i + 4 == heads:
            send_maps(1)
        velocity += attend(mapped(features, 0, slots), keys, 0, slots)
    left("state")
    pair_state[:, :C] = advance(pair_state[:, :C], velocity[:, C:], pair_state[:, C:], start)
    tokens[1, head] = token_features(pair_state[:, :C], in_weight_bf, in_bias)
    send_plane(4, lambda peer: tokens.at[1, head], lambda slot: tokens.at[1, slot])
    arrived(("plane", 3))
    slots = [peer_at(offset) for offset in near_first]
    queries = mapped(tokens[1, head, own_rows, :], 1, slots)
    arrived(("plane", 4))

    keys = tokens[1].reshape(heads * both, 128)
    velocity = jnp.zeros((own, 128), F32)
    for i in range(0, heads, 8):
        velocity += attend(queries[i * own:(i + 8) * own], keys, 1, slots[i:i + 8])
    velocity = velocity[:, C:]
    loads["noise1"].wait()
    latent_out[0] = advance(pair_state[own_rows, :C], velocity, noise1[...], start + 1)
    velocity_out[0] = velocity

    for name in list(leaving):
        left(name)


def shards(groups, heads):
    def run(
        latent, step_noise, start_index, mod_table, in_weight, in_bias,
        base_weight, factor_store, block_order, out_weight,
    ):
        own = latent.shape[1]
        block_rows = (factor_store.shape[0] + 15) // 16 * 16
        total = (D // 128 + heads) * 16
        vmem = pl.BlockSpec(memory_space=pltpu.VMEM)
        anywhere = pl.BlockSpec(memory_space=pl.ANY)
        return pl.pallas_call(
            functools.partial(kernel, groups, heads),
            out_shape=(
                jax.ShapeDtypeStruct(latent.shape, F32),
                jax.ShapeDtypeStruct(latent.shape, F32),
            ),
            in_specs=[
                pl.BlockSpec(memory_space=pltpu.SMEM),
                *[anywhere] * 9,
            ],
            out_specs=(vmem, vmem),
            scratch_shapes=[
                pltpu.VMEM(mod_table.shape, F32),
                pltpu.VMEM(in_weight.shape, BF16),
                pltpu.VMEM((1, D), F32),
                pltpu.VMEM(base_weight.shape, BF16),
                pltpu.VMEM(factor_store.shape, BF16),
                pltpu.VMEM((1, block_order.shape[0]), jnp.int32),
                pltpu.VMEM((own, C), F32),
                pltpu.VMEM((own, C), F32),
                pltpu.VMEM((own, C), F32),
                pltpu.VMEM(out_weight.shape, BF16),
                pltpu.VMEM((2 * own, 128), F32),
                pltpu.VMEM((2, 32, 128), BF16),
                pltpu.VMEM((2, groups // 2, block_rows, 256), BF16),
                pltpu.VMEM((total, 256), BF16),
                pltpu.VMEM((total, 256), BF16),
                pltpu.VMEM((STEPS, 128, D), BF16),
                pltpu.VMEM((STEPS, 128, 3 * HD), F32),
                pltpu.VMEM((STEPS, ROWS, 3 * HD), BF16),
                pltpu.VMEM((STEPS, ROWS, 3 * HD), BF16),
                pltpu.VMEM((heads, 16, 384), BF16),
                pltpu.VMEM((heads, 16, 384), BF16),
                pltpu.VMEM((STEPS, heads, 2 * own, 128), BF16),
                pltpu.VMEM((STEPS, MAP_ROWS, 128), BF16),
                pltpu.VMEM((STEPS, heads, 128, 128), BF16),
                pltpu.SemaphoreType.DMA((10,)),
                pltpu.SemaphoreType.DMA((groups // 2,)),
                pltpu.SemaphoreType.DMA((groups // 2,)),
                pltpu.SemaphoreType.DMA((5,)),
                pltpu.SemaphoreType.DMA((5,)),
                pltpu.SemaphoreType.DMA((5, heads)),
                pltpu.SemaphoreType.DMA((5, heads)),
                pltpu.SemaphoreType.REGULAR,
            ],
            compiler_params=pltpu.CompilerParams(
                collective_id=0, has_side_effects=True, vmem_limit_bytes=63 * 1024 * 1024
            ),
        )(
            start_index, latent, step_noise, mod_table, in_weight, in_bias.reshape(1, -1),
            base_weight, factor_store, block_order.reshape(1, -1), out_weight,
        )

    return run


def solution(mesh):
    in_specs = (
        P("grp", "seq", None),
        P("grp", None, "seq", None),
        P("grp"),
        P(),
        P(),
        P(),
        P(None, "seq", None, None),
        P("grp", None),
        P(),
        P("seq", None),
    )
    out_specs = (P("grp", "seq", None), P("grp", "seq", None))
    run = shards(mesh.shape["grp"], mesh.shape["seq"] // 2)
    return jax.shard_map(run, mesh=mesh, in_specs=in_specs, out_specs=out_specs, check_vma=False)
```

```python
import functools
import math

import jax
import jax.numpy as jnp
from jax import lax
from jax.experimental import pallas as pl
from jax.experimental.pallas import tpu as pltpu
from jax.sharding import PartitionSpec as P

D = 3072
C = 64
HD = 128
RANK = 64
BW = 64
TSTEPS = 10
STEPS = 2
MESH = pl.DeviceIdType.MESH
F32 = jnp.float32
BF16 = jnp.bfloat16
QUERY = 64
KEY = 80
ROWS = 80
MAP_ROWS = 96
NT = (((1,), (1,)), ((), ()))
SIDE = 4
OFFSETS = (
    (2, 2), (2, 1), (2, 3), (1, 2), (3, 2), (1, 1), (3, 3), (1, 3), (3, 1),
    (2, 0), (0, 2), (1, 0), (3, 0), (0, 1), (0, 3),
)


def dot(a, b, dims=(((1,), (0,)), ((), ()))):
    return lax.dot_general(a, b, dims, preferred_element_type=F32)


def exact_dot(a, b, dims=(((1,), (0,)), ((), ()))):
    return lax.dot_general(
        a, b, dims, preferred_element_type=F32, precision=lax.Precision.HIGHEST
    )


def sigma_at(index):
    remaining = 1.0 - index.astype(F32) / TSTEPS
    return 3.0 * remaining / (1.0 + 2.0 * remaining)


def plan(index):
    sigma_now = sigma_at(index)
    sigma_step = sigma_at(index + 1) - sigma_now
    spread = 0.7 * jnp.sqrt(sigma_now / (1.0 - sigma_now))
    return (sigma_now, sigma_step, spread)


def advance(state, velocity, noise, index):
    sigma_now, sigma_step, spread = plan(jnp.full(state.shape, index, jnp.int32))
    return (
        state * (1.0 + spread * spread / (2.0 * sigma_now) * sigma_step)
        + velocity * (1.0 + spread * spread * (1.0 - sigma_now) / (2.0 * sigma_now)) * sigma_step
        + spread * jnp.sqrt(-sigma_step) * noise
    )


def token_features(state, in_weight, in_bias):
    latent_in = state.astype(BF16)
    hidden = dot(latent_in, in_weight) + in_bias
    average = jnp.mean(hidden, axis=-1, keepdims=True)
    centred = hidden - average
    variance = jnp.mean(centred * centred, axis=-1, keepdims=True)
    scale = lax.rsqrt(variance + 1e-06)
    scaled = latent_in.astype(F32) * scale
    high = scale.astype(BF16).astype(F32)
    lane = lax.broadcasted_iota(jnp.int32, scaled.shape, 1)
    entry = jnp.where(lane < 2 * (KEY - QUERY), lane & (KEY - QUERY - 1), 3)
    rest = jnp.where(
        entry == 0, high, jnp.where(entry == 1, 1.0, jnp.where(entry == 2, scale - high, 0.0))
    )
    return jnp.concatenate([scaled, rest], axis=1).astype(BF16)


def kernel(
    groups, heads,
    start_ref, latent_hbm, noise_hbm, mod_hbm, win_hbm, bias_hbm, base_hbm, fac_hbm, order_hbm, wout_hbm,
    result,
    mod, win, bias_ref, base, fac_ref, order_ref, latent0, noise0, noise1, wout_half,
    pair_state, wout, store, perm_even, perm_odd, folded,
    own_part, part_out, part_in, rank_out, rank_in, tokens, maps_out, maps_in,
    load_sem, col_send, col_recv, pair_send, pair_recv, plane_send, plane_recv, ready,
):
    g = lax.axis_index("grp")
    s = lax.axis_index("seq")
    core, zlo = g % 2, g // 2
    zcount = groups // 2
    head, half = s // 2, s % 2
    own = latent_hbm.shape[1]
    both = 2 * own
    half_d = D // 2
    store_rows = fac_hbm.shape[0]
    block_rows = store.shape[2]
    pairs = D // 128
    per_member = 2 * (pairs + heads)

    sibling = (g + 1 - 2 * core, s)
    partner = (g, s + 1 - 2 * half)

    def column_target(j):
        return jnp.where(zlo < zcount // 2, zcount - 1 - j, j)

    def column(other):
        return (other * 2 + core, s)

    def peer_at(offset):
        dx, dy = offset
        return (head // SIDE + dx) % SIDE * SIDE + (head % SIDE + dy) % SIDE

    def plane(h):
        return (g, h * 2 + half)

    loads = {
        name: pltpu.make_async_copy(src, dst, load_sem.at[i])
        for i, (name, src, dst) in enumerate(
            [
                ("in_weight", win_hbm, win),
                ("table", mod_hbm, mod),
                ("in_bias", bias_hbm, bias_ref),
                ("base", base_hbm, base),
                ("factors", fac_hbm, fac_ref),
                ("latent", latent_hbm.at[0], latent0),
                ("noise0", noise_hbm.at[0, 0], noise0),
                ("out_weight", wout_hbm, wout_half),
                ("order", order_hbm, order_ref),
                ("noise1", noise_hbm.at[0, 1], noise1),
            ]
        )
    }
    barrier = pltpu.get_barrier_semaphore()

    def greet(device):
        pl.semaphore_signal(barrier, inc=1, device_id=device, device_id_type=MESH)

    @pl.when(half == 0)
    def _():
        greet(partner)

    for j in range(zcount):
        other = column_target(j)

        @pl.when(other != zlo)
        def _():
            greet(column(other))

    for offset in OFFSETS:
        greet(plane(peer_at(offset)))
    greet(sibling)
    for load in loads.values():
        load.start()

    arriving, leaving = {}, {}

    start = start_ref[0]
    for name in ("in_weight", "in_bias", "table"):
        loads[name].wait()
    in_weight = win[...].astype(F32)
    in_bias = bias_ref[...]
    weight_centred = in_weight - jnp.mean(in_weight, axis=-1, keepdims=True)
    bias_centred = in_bias - jnp.mean(in_bias, axis=-1, keepdims=True)
    extra_row = lax.broadcasted_iota(jnp.int32, (16, D), 0)
    for step in range(STEPS):
        shift = mod[pl.ds(start + step, 1), :D]
        gain = 1.0 + mod[pl.ds(start + step, 1), D:]
        folded[step, :64, :] = (weight_centred * gain).astype(BF16)
        is_bias = (extra_row == 0) | (extra_row == 2)
        extra = jnp.where(is_bias, bias_centred * gain, jnp.where(extra_row == 1, shift, 0.0))
        folded[step, 64:80, :] = extra.astype(BF16)
        folded[step, 80:, :] = jnp.zeros((48, D), BF16)

    loads["base"].wait()
    half_lanes = pl.ds(pl.multiple_of(half * half_d, 128), half_d)
    extras = [[None] * 3 for _ in range(STEPS)]
    for member in range(3):
        part = dot(folded[:, :, half_lanes].reshape(STEPS * 128, half_d), base[member, 0])
        for step in range(STEPS):
            piece = part[step * 128:(step + 1) * 128]
            own_part[step, :, member * HD:(member + 1) * HD] = piece
            part_out[step, member * QUERY:(member + 1) * QUERY, :] = piece[:QUERY].astype(BF16)
            extras[step][member] = piece[QUERY:QUERY + 2]
    for step in range(STEPS):
        rest = jnp.concatenate(extras[step] + [jnp.zeros((10, HD), F32)], axis=0)
        part_out[step, 3 * QUERY:, :] = rest.astype(BF16)

    loads["factors"].wait()
    store[core, zlo] = jnp.zeros(store.shape[2:], BF16)
    lanes = pl.ds(pl.multiple_of(head * 256, 256), 256)
    store[core, zlo, :store_rows, :] = fac_ref[:, lanes]
    for name in ("latent", "noise0", "out_weight"):
        loads[name].wait()
    own_rows = pl.ds(pl.multiple_of(half * own, own), own)
    other_rows = pl.ds(pl.multiple_of((1 - half) * own, own), own)
    pair_state[own_rows, :] = jnp.concatenate([latent0[...], noise0[...]], axis=1)
    packed = wout_half[...].astype(F32)
    wout[half] = jnp.concatenate([packed[:32], packed[32:]], axis=1).astype(BF16)
    for step in range(STEPS):
        maps_in[step, :, MAP_ROWS:, :] = jnp.zeros((heads, 128 - MAP_ROWS, 128), BF16)

    pl.semaphore_wait(barrier, zcount - 1 + 1 + heads - 1 + half)

    def arrived(name):
        arriving.pop(name)()

    def left(name):
        leaving.pop(name)()

    def column_copy(slot, other):
        place = store.at[core, slot]
        return pltpu.make_async_remote_copy(
            src_ref=place, dst_ref=place,
            send_sem=col_send.at[other], recv_sem=col_recv.at[slot],
            device_id=column(other), device_id_type=MESH,
        )

    def each_column(action):
        for j in range(zcount):
            other = column_target(j)

            @pl.when(other != zlo)
            def _():
                action(other)

    def pair_copy(i, src, dst, device=partner):
        return pltpu.make_async_remote_copy(
            src_ref=src, dst_ref=dst,
            send_sem=pair_send.at[i], recv_sem=pair_recv.at[i],
            device_id=device, device_id_type=MESH,
        )

    def exchange(name, i, out, into, device=partner):
        copy = pair_copy(i, out, out, device)
        copy.start()
        arriving[name] = pair_copy(i, into, into, device).wait_recv
        leaving[name] = copy.wait_send

    each_column(lambda other: column_copy(zlo, other).start())
    arriving["column"] = lambda: each_column(lambda other: column_copy(other, other).wait_recv())
    leaving["column"] = lambda: each_column(lambda other: column_copy(zlo, other).wait_send())
    state_copy = pair_copy(0, pair_state.at[own_rows], pair_state.at[own_rows])
    wout_copy = pair_copy(1, wout.at[half], wout.at[half])
    part_copies = [pair_copy(3 + step, part_out.at[step], part_in.at[step]) for step in range(STEPS)]

    def start_pair():
        part_copies[0].start()
        wout_copy.start()
        state_copy.start()

    @pl.when(half == 1)
    def _():
        pl.semaphore_signal(ready, inc=1, device_id=partner, device_id_type=MESH)
        start_pair()


    def plane_copy(kind, src, dst, peer, slot):
        return pltpu.make_async_remote_copy(
            src_ref=src, dst_ref=dst,
            send_sem=plane_send.at[kind, peer], recv_sem=plane_recv.at[kind, slot],
            device_id=plane(peer), device_id_type=MESH,
        )

    def send_plane(kind, src_of, place_of):
        def receive(offsets=OFFSETS):
            for offset in offsets:
                peer = peer_at(offset)
                plane_copy(kind, src_of(peer), place_of(peer), peer, peer).wait_recv()

        def finish():
            for offset in OFFSETS:
                peer = peer_at(offset)
                plane_copy(kind, src_of(peer), place_of(head), peer, head).wait_send()

        for offset in OFFSETS:
            peer = peer_at(offset)
            plane_copy(kind, src_of(peer), place_of(head), peer, head).start()
        arriving["plane", kind] = receive
        leaving["plane", kind] = finish
        return receive

    stored = zcount * 2 * store_rows
    row = lax.broadcasted_iota(jnp.int32, (stored, 256), 0)
    col = lax.broadcasted_iota(jnp.int32, (stored, 256), 1)
    in_block = col % block_rows
    slot = col // block_rows
    shard = slot % zcount * 2 + slot // zcount
    source = jnp.where(in_block < store_rows, shard * store_rows + in_block, -1)
    place = (row == source).astype(F32).astype(BF16)
    loads["order"].wait()
    order = jnp.broadcast_to((order_ref[...] + 1).astype(F32), (16, stored)).astype(BF16)
    order = dot(order, place)[0:1].astype(jnp.int32) - 1
    total = (pairs + heads) * 16
    line = lax.broadcasted_iota(jnp.int32, (total, 256), 0)
    entry = line & 15
    member_of = entry - 3 * ((entry * 11) >> 5)
    target = jnp.where(entry < 12, member_of * per_member + 2 * (line >> 4), -8)
    perm_even[...] = (target == order).astype(F32).astype(BF16)
    perm_odd[...] = (target + 1 == order).astype(F32).astype(BF16)

    arrived("column")
    exchange("sibling", 2, store.at[core], store.at[1 - core], sibling)
    arrived("sibling")
    blocks = store[...].reshape(256, 256)
    even = dot(perm_even[...], blocks)
    odd = dot(perm_odd[...], blocks)
    lane = lax.broadcasted_iota(jnp.int32, (total, 128), 1)
    entry = lax.broadcasted_iota(jnp.int32, (total, 128), 0) & 15
    rank = (entry * 11) >> 5
    even = jnp.where(rank < 2, even[:, :128], even[:, 128:])
    odd = jnp.where(rank < 2, odd[:, :128], odd[:, 128:])
    first = (rank & 1) == 0
    spread = jnp.where(
        lane < 64,
        jnp.where(first, even, pltpu.roll(even, 64, 1)),
        jnp.where(first, pltpu.roll(odd, 64, 1), odd),
    ).astype(BF16)
    lower = jnp.concatenate([spread[i * 16:(i + 1) * 16] for i in range(pairs)], axis=1)
    inner = [dot(lower, folded[step], NT).astype(BF16) for step in range(STEPS)]
    for other in range(heads):
        rank_out[other, :, 0:128] = inner[0]
        rank_out[other, :, 128:256] = inner[1]
        rank_out[other, :, 256:384] = spread[(pairs + other) * 16:(pairs + other + 1) * 16]
    rank_in[head] = rank_out[head]
    send_plane(0, lambda peer: rank_out.at[peer], lambda slot: rank_in.at[slot])

    @pl.when(half == 0)
    def _():
        pl.semaphore_wait(ready, 1)
        start_pair()

    part_copies[1].start()
    place = pair_state.at[other_rows]
    arriving["state"] = pair_copy(0, place, place).wait_recv
    place = wout.at[1 - half]
    arriving["out_weight"] = pair_copy(1, place, place).wait_recv
    leaving["state"] = state_copy.wait_send
    leaving["out_weight"] = wout_copy.wait_send
    for step in range(STEPS):
        arriving["part", step] = part_copies[step].wait_recv
        leaving["part", step] = part_copies[step].wait_send

    arrived("state")
    in_weight_bf = win[...]
    tokens[0, head] = token_features(pair_state[:, :C], in_weight_bf, in_bias)
    send_plane(1, lambda peer: tokens.at[0, head], lambda slot: tokens.at[0, slot])

    arrived(("plane", 0))
    ranks = rank_in[...].reshape(heads * 16, 384)
    entry = lax.broadcasted_iota(jnp.int32, (heads * 16, HD), 0) & 15
    member_of = entry - 3 * ((entry * 11) >> 5)
    upper = ranks[:, 256:].astype(F32)
    upper = jnp.concatenate(
        [jnp.where(member_of == member, upper, 0.0) for member in range(3)], axis=1
    ).astype(BF16)
    low_rank = dot(ranks[:, :256].astype(F32).T.astype(BF16), upper)
    arrived("out_weight")
    sides = [wout[i].astype(F32) for i in range(2)]
    out_weight = jnp.concatenate(
        [side[:, i * C:(i + 1) * C] for side in sides for i in range(2)], axis=0
    )
    got_maps = []

    def make_maps(step):
        arrived(("part", step))
        received = part_in[step].astype(F32)
        rest = received[3 * QUERY:]
        received = jnp.concatenate(
            [
                jnp.concatenate(
                    [
                        received[member * QUERY:(member + 1) * QUERY],
                        rest[2 * member:2 * member + 2],
                        rest[2 * member:2 * member + 1],
                        jnp.zeros((128 - QUERY - 3, HD), F32),
                    ],
                    axis=0,
                )
                for member in range(3)
            ],
            axis=1,
        )
        full = own_part[step] + received + low_rank[step * 128:(step + 1) * 128]
        to_score = HD ** (-0.5) * math.log2(math.e)
        queries, keys = full[:, :HD] * to_score, full[:, HD:2 * HD]
        score_map = exact_dot(queries[:ROWS], keys[:QUERY], NT)
        other_columns = exact_dot(keys[QUERY:ROWS], queries, NT)
        value_map = exact_dot(full[:ROWS, 2 * HD:], out_weight)
        maps_out[step, :ROWS, :] = jnp.concatenate([score_map, value_map], axis=1).astype(BF16)
        maps_out[step, ROWS:, :] = other_columns.astype(BF16)
        maps_in[step, head, :MAP_ROWS, :] = maps_out[step]

    def send_maps(step):
        got_maps.append(
            send_plane(
                2 + step,
                lambda peer: maps_out.at[step],
                lambda slot: maps_in.at[step, slot, pl.ds(0, MAP_ROWS)],
            )
        )

    make_maps(0)
    send_maps(0)
    make_maps(1)

    def first_lanes(features):
        lane = lax.broadcasted_iota(jnp.int32, features.shape, 1)
        return jnp.where(lane < KEY, features, jnp.zeros_like(features))

    def mapped(features, step, slots):
        features = first_lanes(features)
        lane = lax.broadcasted_iota(jnp.int32, features.shape, 1)
        result = []
        for slot in slots:
            maps = maps_in[step, slot]
            columns, others = dot(features, maps), dot(features, maps, NT)
            result.append(jnp.where(lane < QUERY, columns, jnp.where(lane < KEY, 0.0, others)))
        return jnp.concatenate(result, axis=0).astype(BF16)

    def attend(queries, keys, step, slots):
        count = queries.shape[0] // len(slots)
        exponent = jnp.exp2(dot(queries, keys, NT))
        weights = exponent * (1.0 / jnp.sum(exponent, axis=-1, keepdims=True))
        attended = first_lanes(dot(weights.astype(BF16), keys)).astype(BF16)
        sides = jnp.concatenate(
            [attended[i * count:(i + 1) * count] for i in range(len(slots))], axis=1
        )
        return dot(sides, jnp.concatenate([maps_in[step, slot] for slot in slots], axis=0))

    near_first = ((0, 0),) + OFFSETS[::-1]

    arrived(("plane", 1))
    keys = tokens[0].reshape(heads * both, 128)
    features = tokens[0, head]
    arriving.pop(("plane", 2))
    velocity = jnp.zeros((both, 128), F32)
    for i in range(0, heads, 4):
        offsets = near_first[i:i + 4]
        got_maps[0](offsets[1:] if i == 0 else offsets)
        slots = [peer_at(offset) for offset in offsets]
        if i == 4:
            send_maps(1)
        velocity += attend(mapped(features, 0, slots), keys, 0, slots)
    left("state")
    pair_state[:, :C] = advance(pair_state[:, :C], velocity[:, C:], pair_state[:, C:], start)
    tokens[1, head] = token_features(pair_state[:, :C], in_weight_bf, in_bias)
    send_plane(4, lambda peer: tokens.at[1, head], lambda slot: tokens.at[1, slot])
    arrived(("plane", 3))
    slots = [peer_at(offset) for offset in near_first]
    queries = mapped(tokens[1, head, own_rows, :], 1, slots)
    arrived(("plane", 4))

    keys = tokens[1].reshape(heads * both, 128)
    velocity = jnp.zeros((own, 128), F32)
    for i in range(0, heads, 8):
        velocity += attend(queries[i * own:(i + 8) * own], keys, 1, slots[i:i + 8])
    velocity = velocity[:, C:]
    loads["noise1"].wait()
    latent = advance(pair_state[own_rows, :C], velocity, noise1[...], start + 1)
    result[0] = jnp.concatenate([latent, velocity], axis=1)

    for name in list(leaving):
        left(name)


def shards(groups, heads):
    def run(
        latent, step_noise, start_index, mod_table, in_weight, in_bias,
        base_weight, factor_store, block_order, out_weight,
    ):
        own = latent.shape[1]
        block_rows = (factor_store.shape[0] + 15) // 16 * 16
        total = (D // 128 + heads) * 16
        vmem = pl.BlockSpec(memory_space=pltpu.VMEM)
        anywhere = pl.BlockSpec(memory_space=pl.ANY)
        result = pl.pallas_call(
            functools.partial(kernel, groups, heads),
            out_shape=jax.ShapeDtypeStruct((1, own, 2 * C), F32),
            in_specs=[
                pl.BlockSpec(memory_space=pltpu.SMEM),
                *[anywhere] * 9,
            ],
            out_specs=vmem,
            scratch_shapes=[
                pltpu.VMEM(mod_table.shape, F32),
                pltpu.VMEM(in_weight.shape, BF16),
                pltpu.VMEM((1, D), F32),
                pltpu.VMEM(base_weight.shape, BF16),
                pltpu.VMEM(factor_store.shape, BF16),
                pltpu.VMEM((1, block_order.shape[0]), jnp.int32),
                pltpu.VMEM((own, C), F32),
                pltpu.VMEM((own, C), F32),
                pltpu.VMEM((own, C), F32),
                pltpu.VMEM(out_weight.shape, BF16),
                pltpu.VMEM((2 * own, 128), F32),
                pltpu.VMEM((2, 32, 128), BF16),
                pltpu.VMEM((2, groups // 2, block_rows, 256), BF16),
                pltpu.VMEM((total, 256), BF16),
                pltpu.VMEM((total, 256), BF16),
                pltpu.VMEM((STEPS, 128, D), BF16),
                pltpu.VMEM((STEPS, 128, 3 * HD), F32),
                pltpu.VMEM((STEPS, 3 * QUERY + 16, HD), BF16),
                pltpu.VMEM((STEPS, 3 * QUERY + 16, HD), BF16),
                pltpu.VMEM((heads, 16, 384), BF16),
                pltpu.VMEM((heads, 16, 384), BF16),
                pltpu.VMEM((STEPS, heads, 2 * own, 128), BF16),
                pltpu.VMEM((STEPS, MAP_ROWS, 128), BF16),
                pltpu.VMEM((STEPS, heads, 128, 128), BF16),
                pltpu.SemaphoreType.DMA((10,)),
                pltpu.SemaphoreType.DMA((groups // 2,)),
                pltpu.SemaphoreType.DMA((groups // 2,)),
                pltpu.SemaphoreType.DMA((5,)),
                pltpu.SemaphoreType.DMA((5,)),
                pltpu.SemaphoreType.DMA((5, heads)),
                pltpu.SemaphoreType.DMA((5, heads)),
                pltpu.SemaphoreType.REGULAR,
            ],
            compiler_params=pltpu.CompilerParams(
                collective_id=0, has_side_effects=True, vmem_limit_bytes=63 * 1024 * 1024
            ),
        )(
            start_index, latent, step_noise, mod_table, in_weight, in_bias.reshape(1, -1),
            base_weight, factor_store, block_order.reshape(1, -1), out_weight,
        )
        return result[:, :, :C], result[:, :, C:]

    return run


def solution(mesh):
    in_specs = (
        P("grp", "seq", None),
        P("grp", None, "seq", None),
        P("grp"),
        P(),
        P(),
        P(),
        P(None, "seq", None, None),
        P("grp", None),
        P(),
        P("seq", None),
    )
    out_specs = (P("grp", "seq", None), P("grp", "seq", None))
    run = shards(mesh.shape["grp"], mesh.shape["seq"] // 2)
    return jax.shard_map(run, mesh=mesh, in_specs=in_specs, out_specs=out_specs, check_vma=False)
```

```python
import functools
import math

import jax
import jax.numpy as jnp
from jax import lax
from jax.experimental import pallas as pl
from jax.experimental.pallas import tpu as pltpu
from jax.sharding import PartitionSpec as P

D = 3072
C = 64
HD = 128
RANK = 64
BW = 64
TSTEPS = 10
STEPS = 2
MESH = pl.DeviceIdType.MESH
F32 = jnp.float32
BF16 = jnp.bfloat16
QUERY = 64
KEY = 80
ROWS = 80
MAP_ROWS = 96
NT = (((1,), (1,)), ((), ()))
SIDE = 4
OFFSETS = (
    (2, 2), (2, 1), (2, 3), (1, 2), (3, 2), (1, 1), (3, 3), (1, 3), (3, 1),
    (2, 0), (0, 2), (1, 0), (3, 0), (0, 1), (0, 3),
)


def dot(a, b, dims=(((1,), (0,)), ((), ()))):
    return lax.dot_general(a, b, dims, preferred_element_type=F32)


def exact_dot(a, b, dims=(((1,), (0,)), ((), ()))):
    return lax.dot_general(
        a, b, dims, preferred_element_type=F32, precision=lax.Precision.HIGHEST
    )


def sigma_at(index):
    remaining = 1.0 - index.astype(F32) / TSTEPS
    return 3.0 * remaining / (1.0 + 2.0 * remaining)


def plan(index):
    sigma_now = sigma_at(index)
    sigma_step = sigma_at(index + 1) - sigma_now
    spread = 0.7 * jnp.sqrt(sigma_now / (1.0 - sigma_now))
    return (sigma_now, sigma_step, spread)


def carried(state, noise, index):
    sigma_now, sigma_step, spread = plan(jnp.full(state.shape, index, jnp.int32))
    return (
        state * (1.0 + spread * spread / (2.0 * sigma_now) * sigma_step)
        + spread * jnp.sqrt(-sigma_step) * noise
    )


def added(velocity, index):
    sigma_now, sigma_step, spread = plan(jnp.full(velocity.shape, index, jnp.int32))
    return velocity * (1.0 + spread * spread * (1.0 - sigma_now) / (2.0 * sigma_now)) * sigma_step


def pack(rows):
    count = rows.shape[0] // 2
    return jnp.concatenate([rows[:count], rows[count:]], axis=1)


def unpack(rows):
    return jnp.concatenate([rows[:, :64], rows[:, 64:]], axis=0)


def token_features(latent_in, in_weight, in_bias):
    hidden = dot(latent_in, in_weight) + in_bias
    average = jnp.mean(hidden, axis=-1, keepdims=True)
    centred = hidden - average
    variance = jnp.mean(centred * centred, axis=-1, keepdims=True)
    scale = lax.rsqrt(variance + 1e-06)
    scaled = latent_in.astype(F32) * scale
    high = scale.astype(BF16).astype(F32)
    lane = lax.broadcasted_iota(jnp.int32, scaled.shape, 1)
    entry = jnp.where(lane < 2 * (KEY - QUERY), lane & (KEY - QUERY - 1), 3)
    rest = jnp.where(
        entry == 0, high, jnp.where(entry == 1, 1.0, jnp.where(entry == 2, scale - high, 0.0))
    )
    return jnp.concatenate([scaled, rest], axis=1).astype(BF16)


def kernel(
    groups, heads,
    start_ref, latent_hbm, noise_hbm, mod_hbm, win_hbm, bias_hbm, base_hbm, fac_hbm, order_hbm, wout_hbm,
    result,
    mod, win, bias_ref, base, fac_ref, order_ref, latent0, noise0, noise1, wout_half,
    hello, carry, state, store, perm_even, perm_odd, folded,
    own_part, part_out, part_in, rank_out, rank_in, tokens, maps_out, maps_in,
    load_sem, col_send, col_recv, pair_send, pair_recv, plane_send, plane_recv, ready, heard,
):
    g = lax.axis_index("grp")
    s = lax.axis_index("seq")
    core, zlo = g % 2, g // 2
    zcount = groups // 2
    head, half = s // 2, s % 2
    own = latent_hbm.shape[1]
    both = 2 * own
    half_d = D // 2
    store_rows = fac_hbm.shape[0]
    block_rows = store.shape[2]
    pairs = D // 128
    per_member = 2 * (pairs + heads)

    sibling = (g + 1 - 2 * core, s)
    partner = (g, s + 1 - 2 * half)

    def column_target(j):
        return jnp.where(zlo < zcount // 2, zcount - 1 - j, j)

    def column(other):
        return (other * 2 + core, s)

    def peer_at(offset):
        dx, dy = offset
        return (head // SIDE + dx) % SIDE * SIDE + (head % SIDE + dy) % SIDE

    def plane(h):
        return (g, h * 2 + half)

    loads = {
        name: pltpu.make_async_copy(src, dst, load_sem.at[i])
        for i, (name, src, dst) in enumerate(
            [
                ("factors", fac_hbm, fac_ref),
                ("in_weight", win_hbm, win),
                ("table", mod_hbm, mod),
                ("in_bias", bias_hbm, bias_ref),
                ("base", base_hbm, base),
                ("latent", latent_hbm.at[0], latent0),
                ("noise0", noise_hbm.at[0, 0], noise0),
                ("out_weight", wout_hbm, wout_half),
                ("order", order_hbm, order_ref),
                ("noise1", noise_hbm.at[0, 1], noise1),
            ]
        )
    }
    barrier = pltpu.get_barrier_semaphore()

    def greet(device):
        pl.semaphore_signal(barrier, inc=1, device_id=device, device_id_type=MESH)

    @pl.when(half == 0)
    def _():
        greet((zlo * 2, s + 1))

    for j in range(zcount):
        other = column_target(j)

        @pl.when(other != zlo)
        def _():
            greet((other * 2 + half, s))

    for offset in OFFSETS:
        greet((zlo * 2 + 1, peer_at(offset) * 2 + half))
    greet(sibling)
    in_columns, in_planes = 2 * (zcount - 1), 2 * (heads - 1)

    for load in loads.values():
        load.start()

    arriving, leaving = {}, {}

    def column_copy(slot, other):
        place = store.at[core, slot]
        return pltpu.make_async_remote_copy(
            src_ref=place, dst_ref=place,
            send_sem=col_send.at[other], recv_sem=col_recv.at[slot],
            device_id=column(other), device_id_type=MESH,
        )

    def each_column(action):
        for j in range(zcount):
            other = column_target(j)

            @pl.when(other != zlo)
            def _():
                action(other)

    @pl.when(core == 0)
    def _():
        pl.semaphore_wait(barrier, 1 + jnp.where(half == 0, in_columns, 2))
        pl.semaphore_signal(heard, inc=1, device_id=sibling, device_id_type=MESH)

    @pl.when(core == 1)
    def _():
        pl.semaphore_wait(heard, 1)

    @pl.when(half == 1)
    def _():
        pl.semaphore_signal(ready, inc=1, device_id=partner, device_id_type=MESH)

    loads["factors"].wait()
    store[core, zlo] = jnp.zeros(store.shape[2:], BF16)
    lanes = pl.ds(pl.multiple_of(head * 256, 256), 256)
    store[core, zlo, :store_rows, :] = fac_ref[:, lanes]

    @pl.when(half == 0)
    def _():
        each_column(lambda other: column_copy(zlo, other).start())

    start = start_ref[0]
    for name in ("in_weight", "in_bias", "table"):
        loads[name].wait()
    in_weight = win[...].astype(F32)
    in_bias = bias_ref[...]
    weight_centred = in_weight - jnp.mean(in_weight, axis=-1, keepdims=True)
    bias_centred = in_bias - jnp.mean(in_bias, axis=-1, keepdims=True)
    extra_row = lax.broadcasted_iota(jnp.int32, (16, D), 0)
    for step in range(STEPS):
        shift = mod[pl.ds(start + step, 1), :D]
        gain = 1.0 + mod[pl.ds(start + step, 1), D:]
        folded[step, :64, :] = (weight_centred * gain).astype(BF16)
        is_bias = (extra_row == 0) | (extra_row == 2)
        extra = jnp.where(is_bias, bias_centred * gain, jnp.where(extra_row == 1, shift, 0.0))
        folded[step, 64:80, :] = extra.astype(BF16)
        folded[step, 80:, :] = jnp.zeros((48, D), BF16)

    loads["base"].wait()
    half_lanes = pl.ds(pl.multiple_of(half * half_d, 128), half_d)
    extras = [[None] * 3 for _ in range(STEPS)]
    for member in range(3):
        part = dot(folded[:, :, half_lanes].reshape(STEPS * 128, half_d), base[member, 0])
        for step in range(STEPS):
            piece = part[step * 128:(step + 1) * 128]
            own_part[step, :, member * HD:(member + 1) * HD] = piece
            part_out[step, member * QUERY:(member + 1) * QUERY, :] = piece[:QUERY].astype(BF16)
            extras[step][member] = piece[QUERY:QUERY + 2]
    for step in range(STEPS):
        rest = jnp.concatenate(extras[step] + [jnp.zeros((10, HD), F32)], axis=0)
        part_out[step, 3 * QUERY:, :] = rest.astype(BF16)

    for name in ("latent", "noise0", "out_weight"):
        loads[name].wait()
    hello[half, :own // 2, :] = pack(latent0[...]).astype(BF16)
    hello[half, own // 2:, :] = pack(wout_half[...].astype(F32)).astype(BF16)
    carry[half] = pack(carried(latent0[...], noise0[...], start))
    own_rows = pl.ds(pl.multiple_of(half * own, own), own)
    for step in range(STEPS):
        maps_in[step, :, MAP_ROWS:, :] = jnp.zeros((heads, 128 - MAP_ROWS, 128), BF16)

    def arrived(name):
        arriving.pop(name)()

    def left(name):
        leaving.pop(name)()

    def pair_copy(i, src, dst, device=partner):
        return pltpu.make_async_remote_copy(
            src_ref=src, dst_ref=dst,
            send_sem=pair_send.at[i], recv_sem=pair_recv.at[i],
            device_id=device, device_id_type=MESH,
        )

    def exchange(name, i, out, into, device=partner):
        copy = pair_copy(i, out, out, device)
        copy.start()
        arriving[name] = pair_copy(i, into, into, device).wait_recv
        leaving[name] = copy.wait_send

    hello_copy = pair_copy(0, hello.at[half], hello.at[half])
    carry_copy = pair_copy(1, carry.at[half], carry.at[half])
    part_copies = [pair_copy(3 + step, part_out.at[step], part_in.at[step]) for step in range(STEPS)]

    def start_pair():
        hello_copy.start()
        part_copies[0].start()

    @pl.when(core == 1)
    def _():
        pl.semaphore_wait(barrier, 1 + in_planes + jnp.where(half == 0, 0, in_columns))
        pl.semaphore_signal(heard, inc=1, device_id=sibling, device_id_type=MESH)

    @pl.when(core == 0)
    def _():
        pl.semaphore_wait(heard, 1)

    @pl.when(half == 1)
    def _():
        each_column(lambda other: column_copy(zlo, other).start())
        start_pair()

    arriving["column"] = lambda: each_column(lambda other: column_copy(other, other).wait_recv())
    leaving["column"] = lambda: each_column(lambda other: column_copy(zlo, other).wait_send())

    def plane_copy(kind, src, dst, peer, slot):
        return pltpu.make_async_remote_copy(
            src_ref=src, dst_ref=dst,
            send_sem=plane_send.at[kind, peer], recv_sem=plane_recv.at[kind, slot],
            device_id=plane(peer), device_id_type=MESH,
        )

    def send_plane(kind, src_of, place_of):
        def receive(offsets=OFFSETS):
            for offset in offsets:
                peer = peer_at(offset)
                plane_copy(kind, src_of(peer), place_of(peer), peer, peer).wait_recv()

        def finish():
            for offset in OFFSETS:
                peer = peer_at(offset)
                plane_copy(kind, src_of(peer), place_of(head), peer, head).wait_send()

        for offset in OFFSETS:
            peer = peer_at(offset)
            plane_copy(kind, src_of(peer), place_of(head), peer, head).start()
        arriving["plane", kind] = receive
        leaving["plane", kind] = finish
        return receive

    stored = zcount * 2 * store_rows
    row = lax.broadcasted_iota(jnp.int32, (stored, 256), 0)
    col = lax.broadcasted_iota(jnp.int32, (stored, 256), 1)
    in_block = col % block_rows
    slot = col // block_rows
    shard = slot % zcount * 2 + slot // zcount
    source = jnp.where(in_block < store_rows, shard * store_rows + in_block, -1)
    place = (row == source).astype(F32).astype(BF16)
    loads["order"].wait()
    order = jnp.broadcast_to((order_ref[...] + 1).astype(F32), (16, stored)).astype(BF16)
    order = dot(order, place)[0:1].astype(jnp.int32) - 1
    total = (pairs + heads) * 16
    line = lax.broadcasted_iota(jnp.int32, (total, 256), 0)
    entry = line & 15
    member_of = entry - 3 * ((entry * 11) >> 5)
    target = jnp.where(entry < 12, member_of * per_member + 2 * (line >> 4), -8)
    perm_even[...] = (target == order).astype(F32).astype(BF16)
    perm_odd[...] = (target + 1 == order).astype(F32).astype(BF16)

    arrived("column")
    exchange("sibling", 2, store.at[core], store.at[1 - core], sibling)

    @pl.when(half == 0)
    def _():
        pl.semaphore_wait(ready, 1)
        start_pair()

    arrived("sibling")
    blocks = store[...].reshape(256, 256)
    even = dot(perm_even[...], blocks)
    odd = dot(perm_odd[...], blocks)
    lane = lax.broadcasted_iota(jnp.int32, (total, 128), 1)
    entry = lax.broadcasted_iota(jnp.int32, (total, 128), 0) & 15
    rank = (entry * 11) >> 5
    even = jnp.where(rank < 2, even[:, :128], even[:, 128:])
    odd = jnp.where(rank < 2, odd[:, :128], odd[:, 128:])
    first = (rank & 1) == 0
    spread = jnp.where(
        lane < 64,
        jnp.where(first, even, pltpu.roll(even, 64, 1)),
        jnp.where(first, pltpu.roll(odd, 64, 1), odd),
    ).astype(BF16)
    lower = jnp.concatenate([spread[i * 16:(i + 1) * 16] for i in range(pairs)], axis=1)
    inner = [dot(lower, folded[step], NT).astype(BF16) for step in range(STEPS)]
    for other in range(heads):
        rank_out[other, :, 0:128] = inner[0]
        rank_out[other, :, 128:256] = inner[1]
        rank_out[other, :, 256:384] = spread[(pairs + other) * 16:(pairs + other + 1) * 16]
    rank_in[head] = rank_out[head]
    send_plane(0, lambda peer: rank_out.at[peer], lambda slot: rank_in.at[slot])

    carry_copy.start()
    part_copies[1].start()
    for name, i, buffer, copy in (("hello", 0, hello, hello_copy), ("carry", 1, carry, carry_copy)):
        arriving[name] = pair_copy(i, buffer.at[1 - half], buffer.at[1 - half]).wait_recv
        leaving[name] = copy.wait_send
    for step in range(STEPS):
        arriving["part", step] = part_copies[step].wait_recv
        leaving["part", step] = part_copies[step].wait_send

    arrived("hello")
    in_weight_bf = win[...]
    latent_in = jnp.concatenate(
        [unpack(hello[i, :own // 2, :].astype(F32)) for i in range(2)], axis=0
    ).astype(BF16)
    tokens[0, head] = token_features(latent_in, in_weight_bf, in_bias)
    send_plane(1, lambda peer: tokens.at[0, head], lambda slot: tokens.at[0, slot])

    arrived(("plane", 0))
    ranks = rank_in[...].reshape(heads * 16, 384)
    entry = lax.broadcasted_iota(jnp.int32, (heads * 16, HD), 0) & 15
    member_of = entry - 3 * ((entry * 11) >> 5)
    upper = ranks[:, 256:].astype(F32)
    upper = jnp.concatenate(
        [jnp.where(member_of == member, upper, 0.0) for member in range(3)], axis=1
    ).astype(BF16)
    low_rank = dot(ranks[:, :256].astype(F32).T.astype(BF16), upper)
    out_weight = jnp.concatenate(
        [unpack(hello[i, own // 2:, :].astype(F32)) for i in range(2)], axis=0
    )
    got_maps = []

    def make_maps(step):
        arrived(("part", step))
        received = part_in[step].astype(F32)
        rest = received[3 * QUERY:]
        received = jnp.concatenate(
            [
                jnp.concatenate(
                    [
                        received[member * QUERY:(member + 1) * QUERY],
                        rest[2 * member:2 * member + 2],
                        rest[2 * member:2 * member + 1],
                        jnp.zeros((128 - QUERY - 3, HD), F32),
                    ],
                    axis=0,
                )
                for member in range(3)
            ],
            axis=1,
        )
        full = own_part[step] + received + low_rank[step * 128:(step + 1) * 128]
        to_score = HD ** (-0.5) * math.log2(math.e)
        queries, keys = full[:, :HD] * to_score, full[:, HD:2 * HD]
        score_map = exact_dot(queries[:ROWS], keys[:QUERY], NT)
        other_columns = exact_dot(keys[QUERY:ROWS], queries, NT)
        value_map = exact_dot(full[:ROWS, 2 * HD:], out_weight)
        maps_out[step, :ROWS, :] = jnp.concatenate([score_map, value_map], axis=1).astype(BF16)
        maps_out[step, ROWS:, :] = other_columns.astype(BF16)
        maps_in[step, head, :MAP_ROWS, :] = maps_out[step]

    def send_maps(step):
        got_maps.append(
            send_plane(
                2 + step,
                lambda peer: maps_out.at[step],
                lambda slot: maps_in.at[step, slot, pl.ds(0, MAP_ROWS)],
            )
        )

    make_maps(0)
    send_maps(0)
    make_maps(1)

    def first_lanes(features):
        lane = lax.broadcasted_iota(jnp.int32, features.shape, 1)
        return jnp.where(lane < KEY, features, jnp.zeros_like(features))

    def mapped(features, step, slots):
        features = first_lanes(features)
        lane = lax.broadcasted_iota(jnp.int32, features.shape, 1)
        result = []
        for slot in slots:
            maps = maps_in[step, slot]
            columns, others = dot(features, maps), dot(features, maps, NT)
            result.append(jnp.where(lane < QUERY, columns, jnp.where(lane < KEY, 0.0, others)))
        return jnp.concatenate(result, axis=0).astype(BF16)

    def attend(queries, keys, step, slots):
        count = queries.shape[0] // len(slots)
        exponent = jnp.exp2(dot(queries, keys, NT))
        weights = exponent * (1.0 / jnp.sum(exponent, axis=-1, keepdims=True))
        attended = first_lanes(dot(weights.astype(BF16), keys)).astype(BF16)
        sides = jnp.concatenate(
            [attended[i * count:(i + 1) * count] for i in range(len(slots))], axis=1
        )
        return dot(sides, jnp.concatenate([maps_in[step, slot] for slot in slots], axis=0))

    near_first = ((0, 0),) + OFFSETS[::-1]

    arrived(("plane", 1))
    keys = tokens[0].reshape(heads * both, 128)
    features = tokens[0, head]
    arriving.pop(("plane", 2))
    velocity = jnp.zeros((both, 128), F32)
    for i in range(0, heads, 4):
        offsets = near_first[i:i + 4]
        got_maps[0](offsets[1:] if i == 0 else offsets)
        slots = [peer_at(offset) for offset in offsets]
        if i == 4:
            send_maps(1)
        velocity += attend(mapped(features, 0, slots), keys, 0, slots)
    arrived("carry")
    carry_rows = jnp.concatenate([unpack(carry[i]) for i in range(2)], axis=0)
    state[...] = carry_rows + added(velocity[:, C:], start)
    tokens[1, head] = token_features(state[...].astype(BF16), in_weight_bf, in_bias)
    send_plane(4, lambda peer: tokens.at[1, head], lambda slot: tokens.at[1, slot])
    arrived(("plane", 3))
    slots = [peer_at(offset) for offset in near_first]
    queries = mapped(tokens[1, head, own_rows, :], 1, slots)
    arrived(("plane", 4))

    keys = tokens[1].reshape(heads * both, 128)
    velocity = jnp.zeros((own, 128), F32)
    for i in range(0, heads, 8):
        velocity += attend(queries[i * own:(i + 8) * own], keys, 1, slots[i:i + 8])
    velocity = velocity[:, C:]
    loads["noise1"].wait()
    latent = carried(state[own_rows, :], noise1[...], start + 1) + added(velocity, start + 1)
    result[0] = jnp.concatenate([latent, velocity], axis=1)

    for name in list(leaving):
        left(name)


def shards(groups, heads):
    def run(
        latent, step_noise, start_index, mod_table, in_weight, in_bias,
        base_weight, factor_store, block_order, out_weight,
    ):
        own = latent.shape[1]
        block_rows = (factor_store.shape[0] + 15) // 16 * 16
        total = (D // 128 + heads) * 16
        vmem = pl.BlockSpec(memory_space=pltpu.VMEM)
        anywhere = pl.BlockSpec(memory_space=pl.ANY)
        result = pl.pallas_call(
            functools.partial(kernel, groups, heads),
            out_shape=jax.ShapeDtypeStruct((1, own, 2 * C), F32),
            in_specs=[
                pl.BlockSpec(memory_space=pltpu.SMEM),
                *[anywhere] * 9,
            ],
            out_specs=vmem,
            scratch_shapes=[
                pltpu.VMEM(mod_table.shape, F32),
                pltpu.VMEM(in_weight.shape, BF16),
                pltpu.VMEM((1, D), F32),
                pltpu.VMEM(base_weight.shape, BF16),
                pltpu.VMEM(factor_store.shape, BF16),
                pltpu.VMEM((1, block_order.shape[0]), jnp.int32),
                pltpu.VMEM((own, C), F32),
                pltpu.VMEM((own, C), F32),
                pltpu.VMEM((own, C), F32),
                pltpu.VMEM(out_weight.shape, BF16),
                pltpu.VMEM((2, own // 2 + 32, 128), BF16),
                pltpu.VMEM((2, own // 2, 128), F32),
                pltpu.VMEM((2 * own, C), F32),
                pltpu.VMEM((2, groups // 2, block_rows, 256), BF16),
                pltpu.VMEM((total, 256), BF16),
                pltpu.VMEM((total, 256), BF16),
                pltpu.VMEM((STEPS, 128, D), BF16),
                pltpu.VMEM((STEPS, 128, 3 * HD), F32),
                pltpu.VMEM((STEPS, 3 * QUERY + 16, HD), BF16),
                pltpu.VMEM((STEPS, 3 * QUERY + 16, HD), BF16),
                pltpu.VMEM((heads, 16, 384), BF16),
                pltpu.VMEM((heads, 16, 384), BF16),
                pltpu.VMEM((STEPS, heads, 2 * own, 128), BF16),
                pltpu.VMEM((STEPS, MAP_ROWS, 128), BF16),
                pltpu.VMEM((STEPS, heads, 128, 128), BF16),
                pltpu.SemaphoreType.DMA((10,)),
                pltpu.SemaphoreType.DMA((groups // 2,)),
                pltpu.SemaphoreType.DMA((groups // 2,)),
                pltpu.SemaphoreType.DMA((5,)),
                pltpu.SemaphoreType.DMA((5,)),
                pltpu.SemaphoreType.DMA((5, heads)),
                pltpu.SemaphoreType.DMA((5, heads)),
                pltpu.SemaphoreType.REGULAR,
                pltpu.SemaphoreType.REGULAR,
            ],
            compiler_params=pltpu.CompilerParams(
                collective_id=0, has_side_effects=True, vmem_limit_bytes=63 * 1024 * 1024
            ),
        )(
            start_index, latent, step_noise, mod_table, in_weight, in_bias.reshape(1, -1),
            base_weight, factor_store, block_order.reshape(1, -1), out_weight,
        )
        return result[:, :, :C], result[:, :, C:]

    return run


def solution(mesh):
    in_specs = (
        P("grp", "seq", None),
        P("grp", None, "seq", None),
        P("grp"),
        P(),
        P(),
        P(),
        P(None, "seq", None, None),
        P("grp", None),
        P(),
        P("seq", None),
    )
    out_specs = (P("grp", "seq", None), P("grp", "seq", None))
    run = shards(mesh.shape["grp"], mesh.shape["seq"] // 2)
    return jax.shard_map(run, mesh=mesh, in_specs=in_specs, out_specs=out_specs, check_vma=False)
```

```python
import functools
import math

import jax
import jax.numpy as jnp
from jax import lax
from jax.experimental import pallas as pl
from jax.experimental.pallas import tpu as pltpu
from jax.sharding import PartitionSpec as P

D = 3072
C = 64
HD = 128
RANK = 64
BW = 64
TSTEPS = 10
STEPS = 2
MESH = pl.DeviceIdType.MESH
F32 = jnp.float32
BF16 = jnp.bfloat16
QUERY = 64
KEY = 80
ROWS = 80
MAP_ROWS = 96
NT = (((1,), (1,)), ((), ()))
SIDE = 4
OFFSETS = (
    (2, 2), (2, 1), (2, 3), (1, 2), (3, 2), (1, 1), (3, 3), (1, 3), (3, 1),
    (2, 0), (0, 2), (1, 0), (3, 0), (0, 1), (0, 3),
)


def dot(a, b, dims=(((1,), (0,)), ((), ()))):
    return lax.dot_general(a, b, dims, preferred_element_type=F32)


def exact_dot(a, b, dims=(((1,), (0,)), ((), ()))):
    return lax.dot_general(
        a, b, dims, preferred_element_type=F32, precision=lax.Precision.HIGHEST
    )


def sigma_at(index):
    remaining = 1.0 - index.astype(F32) / TSTEPS
    return 3.0 * remaining / (1.0 + 2.0 * remaining)


def plan(index):
    sigma_now = sigma_at(index)
    sigma_step = sigma_at(index + 1) - sigma_now
    spread = 0.7 * jnp.sqrt(sigma_now / (1.0 - sigma_now))
    return (sigma_now, sigma_step, spread)


def carried(state, noise, index):
    sigma_now, sigma_step, spread = plan(jnp.full(state.shape, index, jnp.int32))
    return (
        state * (1.0 + spread * spread / (2.0 * sigma_now) * sigma_step)
        + spread * jnp.sqrt(-sigma_step) * noise
    )


def added(velocity, index):
    sigma_now, sigma_step, spread = plan(jnp.full(velocity.shape, index, jnp.int32))
    return velocity * (1.0 + spread * spread * (1.0 - sigma_now) / (2.0 * sigma_now)) * sigma_step


def pack(rows):
    count = rows.shape[0] // 2
    return jnp.concatenate([rows[:count], rows[count:]], axis=1)


def unpack(rows):
    return jnp.concatenate([rows[:, :64], rows[:, 64:]], axis=0)


def token_features(latent_in, in_weight, in_bias):
    hidden = dot(latent_in, in_weight) + in_bias
    average = jnp.mean(hidden, axis=-1, keepdims=True)
    centred = hidden - average
    variance = jnp.mean(centred * centred, axis=-1, keepdims=True)
    scale = lax.rsqrt(variance + 1e-06)
    scaled = latent_in.astype(F32) * scale
    high = scale.astype(BF16).astype(F32)
    lane = lax.broadcasted_iota(jnp.int32, scaled.shape, 1)
    entry = jnp.where(lane < 2 * (KEY - QUERY), lane & (KEY - QUERY - 1), 3)
    rest = jnp.where(
        entry == 0, high, jnp.where(entry == 1, 1.0, jnp.where(entry == 2, scale - high, 0.0))
    )
    return jnp.concatenate([scaled, rest], axis=1).astype(BF16)


def kernel(
    groups, heads,
    start_ref, latent_hbm, noise_hbm, mod_hbm, win_hbm, bias_hbm, base_hbm, fac_hbm, order_hbm, wout_hbm,
    result,
    mod, win, bias_ref, base, fac_ref, order_ref, latent0, noise0, noise1, wout_half,
    hello, carry, state, store, perm_even, perm_odd, folded,
    own_part, part_out, part_in, rank_out, rank_in, tokens, maps_out, maps_in,
    load_sem, col_send, col_recv, pair_send, pair_recv, plane_send, plane_recv, ready, heard,
):
    g = lax.axis_index("grp")
    s = lax.axis_index("seq")
    core, zlo = g % 2, g // 2
    zcount = groups // 2
    head, half = s // 2, s % 2
    own = latent_hbm.shape[1]
    both = 2 * own
    half_d = D // 2
    store_rows = fac_hbm.shape[0]
    block_rows = store.shape[2]
    pairs = D // 128
    per_member = 2 * (pairs + heads)

    sibling = (g + 1 - 2 * core, s)
    partner = (g, s + 1 - 2 * half)

    def column_target(j):
        return jnp.where(zlo < zcount // 2, zcount - 1 - j, j)

    def column(other):
        return (other * 2 + core, s)

    def peer_at(offset):
        dx, dy = offset
        return (head // SIDE + dx) % SIDE * SIDE + (head % SIDE + dy) % SIDE

    def plane(h):
        return (g, h * 2 + half)

    loads = {
        name: pltpu.make_async_copy(src, dst, load_sem.at[i])
        for i, (name, src, dst) in enumerate(
            [
                ("factors", fac_hbm, fac_ref),
                ("in_weight", win_hbm, win),
                ("table", mod_hbm, mod),
                ("in_bias", bias_hbm, bias_ref),
                ("base", base_hbm, base),
                ("latent", latent_hbm.at[0], latent0),
                ("noise0", noise_hbm.at[0, 0], noise0),
                ("out_weight", wout_hbm, wout_half),
                ("order", order_hbm, order_ref),
                ("noise1", noise_hbm.at[0, 1], noise1),
            ]
        )
    }
    loads["factors"].start()

    barrier = pltpu.get_barrier_semaphore()

    def greet(device):
        pl.semaphore_signal(barrier, inc=1, device_id=device, device_id_type=MESH)

    @pl.when(half == 0)
    def _():
        greet((zlo * 2, s + 1))

    for j in range(zcount):
        other = column_target(j)

        @pl.when(other != zlo)
        def _():
            greet((other * 2 + half, s))

    for offset in OFFSETS:
        greet((zlo * 2 + 1, peer_at(offset) * 2 + half))
    greet(sibling)
    in_columns, in_planes = 2 * (zcount - 1), 2 * (heads - 1)

    for name in list(loads)[1:]:
        loads[name].start()

    arriving, leaving = {}, {}

    def column_copy(slot, other):
        place = store.at[core, slot]
        return pltpu.make_async_remote_copy(
            src_ref=place, dst_ref=place,
            send_sem=col_send.at[other], recv_sem=col_recv.at[slot],
            device_id=column(other), device_id_type=MESH,
        )

    def each_column(action):
        for j in range(zcount):
            other = column_target(j)

            @pl.when(other != zlo)
            def _():
                action(other)

    @pl.when(core == 0)
    def _():
        pl.semaphore_wait(barrier, 1 + jnp.where(half == 0, in_columns, 2))
        pl.semaphore_signal(heard, inc=1, device_id=sibling, device_id_type=MESH)

    @pl.when(core == 1)
    def _():
        pl.semaphore_wait(heard, 1)

    @pl.when(half == 1)
    def _():
        pl.semaphore_signal(ready, inc=1, device_id=partner, device_id_type=MESH)

    loads["factors"].wait()
    store[core, zlo] = jnp.zeros(store.shape[2:], BF16)
    lanes = pl.ds(pl.multiple_of(head * 256, 256), 256)
    store[core, zlo, :store_rows, :] = fac_ref[:, lanes]

    @pl.when(half == 0)
    def _():
        each_column(lambda other: column_copy(zlo, other).start())

    start = start_ref[0]
    for name in ("in_weight", "in_bias", "table"):
        loads[name].wait()
    in_weight = win[...].astype(F32)
    in_bias = bias_ref[...]
    weight_centred = in_weight - jnp.mean(in_weight, axis=-1, keepdims=True)
    bias_centred = in_bias - jnp.mean(in_bias, axis=-1, keepdims=True)
    extra_row = lax.broadcasted_iota(jnp.int32, (16, D), 0)
    for step in range(STEPS):
        shift = mod[pl.ds(start + step, 1), :D]
        gain = 1.0 + mod[pl.ds(start + step, 1), D:]
        folded[step, :64, :] = (weight_centred * gain).astype(BF16)
        is_bias = (extra_row == 0) | (extra_row == 2)
        extra = jnp.where(is_bias, bias_centred * gain, jnp.where(extra_row == 1, shift, 0.0))
        folded[step, 64:80, :] = extra.astype(BF16)
        folded[step, 80:, :] = jnp.zeros((48, D), BF16)

    loads["base"].wait()
    half_lanes = pl.ds(pl.multiple_of(half * half_d, 128), half_d)
    extras = [[None] * 3 for _ in range(STEPS)]
    for member in range(3):
        part = dot(folded[:, :, half_lanes].reshape(STEPS * 128, half_d), base[member, 0])
        for step in range(STEPS):
            piece = part[step * 128:(step + 1) * 128]
            own_part[step, :, member * HD:(member + 1) * HD] = piece
            part_out[step, member * QUERY:(member + 1) * QUERY, :] = piece[:QUERY].astype(BF16)
            extras[step][member] = piece[QUERY:QUERY + 2]
    for step in range(STEPS):
        rest = jnp.concatenate(extras[step] + [jnp.zeros((10, HD), F32)], axis=0)
        part_out[step, 3 * QUERY:, :] = rest.astype(BF16)

    for name in ("latent", "noise0", "out_weight"):
        loads[name].wait()
    hello[half, :own // 2, :] = pack(latent0[...]).astype(BF16)
    hello[half, own // 2:, :] = pack(wout_half[...].astype(F32)).astype(BF16)
    carry[half] = pack(carried(latent0[...], noise0[...], start))
    own_rows = pl.ds(pl.multiple_of(half * own, own), own)
    for step in range(STEPS):
        maps_in[step, :, MAP_ROWS:, :] = jnp.zeros((heads, 128 - MAP_ROWS, 128), BF16)

    def arrived(name):
        arriving.pop(name)()

    def left(name):
        leaving.pop(name)()

    def pair_copy(i, src, dst, device=partner):
        return pltpu.make_async_remote_copy(
            src_ref=src, dst_ref=dst,
            send_sem=pair_send.at[i], recv_sem=pair_recv.at[i],
            device_id=device, device_id_type=MESH,
        )

    def exchange(name, i, out, into, device=partner):
        copy = pair_copy(i, out, out, device)
        copy.start()
        arriving[name] = pair_copy(i, into, into, device).wait_recv
        leaving[name] = copy.wait_send

    hello_copy = pair_copy(0, hello.at[half], hello.at[half])
    carry_copy = pair_copy(1, carry.at[half], carry.at[half])
    part_copies = [pair_copy(3 + step, part_out.at[step], part_in.at[step]) for step in range(STEPS)]

    def start_pair():
        hello_copy.start()
        part_copies[0].start()

    def start_late_pair():
        carry_copy.start()
        part_copies[1].start()

    @pl.when(core == 1)
    def _():
        pl.semaphore_wait(barrier, 1 + in_planes + jnp.where(half == 0, 0, in_columns))
        pl.semaphore_signal(heard, inc=1, device_id=sibling, device_id_type=MESH)

    @pl.when(core == 0)
    def _():
        pl.semaphore_wait(heard, 1)

    @pl.when(half == 1)
    def _():
        each_column(lambda other: column_copy(zlo, other).start())
        start_pair()

    arriving["column"] = lambda: each_column(lambda other: column_copy(other, other).wait_recv())
    leaving["column"] = lambda: each_column(lambda other: column_copy(zlo, other).wait_send())

    def plane_copy(kind, src, dst, peer, slot):
        return pltpu.make_async_remote_copy(
            src_ref=src, dst_ref=dst,
            send_sem=plane_send.at[kind, peer], recv_sem=plane_recv.at[kind, slot],
            device_id=plane(peer), device_id_type=MESH,
        )

    def send_plane(kind, src_of, place_of):
        def receive(offsets=OFFSETS):
            for offset in offsets:
                peer = peer_at(offset)
                plane_copy(kind, src_of(peer), place_of(peer), peer, peer).wait_recv()

        def finish():
            for offset in OFFSETS:
                peer = peer_at(offset)
                plane_copy(kind, src_of(peer), place_of(head), peer, head).wait_send()

        for offset in OFFSETS:
            peer = peer_at(offset)
            plane_copy(kind, src_of(peer), place_of(head), peer, head).start()
        arriving["plane", kind] = receive
        leaving["plane", kind] = finish
        return receive

    stored = zcount * 2 * store_rows
    row = lax.broadcasted_iota(jnp.int32, (stored, 256), 0)
    col = lax.broadcasted_iota(jnp.int32, (stored, 256), 1)
    in_block = col % block_rows
    slot = col // block_rows
    shard = slot % zcount * 2 + slot // zcount
    source = jnp.where(in_block < store_rows, shard * store_rows + in_block, -1)
    place = (row == source).astype(F32).astype(BF16)
    loads["order"].wait()
    order = jnp.broadcast_to((order_ref[...] + 1).astype(F32), (16, stored)).astype(BF16)
    order = dot(order, place)[0:1].astype(jnp.int32) - 1
    total = (pairs + heads) * 16
    line = lax.broadcasted_iota(jnp.int32, (total, 256), 0)
    entry = line & 15
    member_of = entry - 3 * ((entry * 11) >> 5)
    target = jnp.where(entry < 12, member_of * per_member + 2 * (line >> 4), -8)
    perm_even[...] = (target == order).astype(F32).astype(BF16)
    perm_odd[...] = (target + 1 == order).astype(F32).astype(BF16)

    arrived("column")
    exchange("sibling", 2, store.at[core], store.at[1 - core], sibling)

    @pl.when(half == 0)
    def _():
        pl.semaphore_wait(ready, 1)
        start_pair()

    @pl.when(half == 1)
    def _():
        start_late_pair()

    arrived("sibling")
    blocks = store[...].reshape(256, 256)
    even = dot(perm_even[...], blocks)
    odd = dot(perm_odd[...], blocks)
    lane = lax.broadcasted_iota(jnp.int32, (total, 128), 1)
    entry = lax.broadcasted_iota(jnp.int32, (total, 128), 0) & 15
    rank = (entry * 11) >> 5
    even = jnp.where(rank < 2, even[:, :128], even[:, 128:])
    odd = jnp.where(rank < 2, odd[:, :128], odd[:, 128:])
    first = (rank & 1) == 0
    spread = jnp.where(
        lane < 64,
        jnp.where(first, even, pltpu.roll(even, 64, 1)),
        jnp.where(first, pltpu.roll(odd, 64, 1), odd),
    ).astype(BF16)
    lower = jnp.concatenate([spread[i * 16:(i + 1) * 16] for i in range(pairs)], axis=1)
    inner = [dot(lower, folded[step], NT).astype(BF16) for step in range(STEPS)]
    for other in range(heads):
        rank_out[other, :, 0:128] = inner[0]
        rank_out[other, :, 128:256] = inner[1]
        rank_out[other, :, 256:384] = spread[(pairs + other) * 16:(pairs + other + 1) * 16]
    rank_in[head] = rank_out[head]
    send_plane(0, lambda peer: rank_out.at[peer], lambda slot: rank_in.at[slot])

    @pl.when(half == 0)
    def _():
        start_late_pair()

    for name, i, buffer, copy in (("hello", 0, hello, hello_copy), ("carry", 1, carry, carry_copy)):
        arriving[name] = pair_copy(i, buffer.at[1 - half], buffer.at[1 - half]).wait_recv
        leaving[name] = copy.wait_send
    for step in range(STEPS):
        arriving["part", step] = part_copies[step].wait_recv
        leaving["part", step] = part_copies[step].wait_send

    arrived("hello")
    in_weight_bf = win[...]
    latent_in = jnp.concatenate(
        [unpack(hello[i, :own // 2, :].astype(F32)) for i in range(2)], axis=0
    ).astype(BF16)
    tokens[0, head] = token_features(latent_in, in_weight_bf, in_bias)
    send_plane(1, lambda peer: tokens.at[0, head], lambda slot: tokens.at[0, slot])

    arrived(("plane", 0))
    ranks = rank_in[...].reshape(heads * 16, 384)
    entry = lax.broadcasted_iota(jnp.int32, (heads * 16, HD), 0) & 15
    member_of = entry - 3 * ((entry * 11) >> 5)
    upper = ranks[:, 256:].astype(F32)
    upper = jnp.concatenate(
        [jnp.where(member_of == member, upper, 0.0) for member in range(3)], axis=1
    ).astype(BF16)
    low_rank = dot(ranks[:, :256].astype(F32).T.astype(BF16), upper)
    out_weight = jnp.concatenate(
        [unpack(hello[i, own // 2:, :].astype(F32)) for i in range(2)], axis=0
    )
    got_maps = []

    def make_maps(step):
        arrived(("part", step))
        received = part_in[step].astype(F32)
        rest = received[3 * QUERY:]
        received = jnp.concatenate(
            [
                jnp.concatenate(
                    [
                        received[member * QUERY:(member + 1) * QUERY],
                        rest[2 * member:2 * member + 2],
                        rest[2 * member:2 * member + 1],
                        jnp.zeros((128 - QUERY - 3, HD), F32),
                    ],
                    axis=0,
                )
                for member in range(3)
            ],
            axis=1,
        )
        full = own_part[step] + received + low_rank[step * 128:(step + 1) * 128]
        to_score = HD ** (-0.5) * math.log2(math.e)
        queries, keys = full[:, :HD] * to_score, full[:, HD:2 * HD]
        score_map = exact_dot(queries[:ROWS], keys[:QUERY], NT)
        other_columns = exact_dot(keys[QUERY:ROWS], queries, NT)
        value_map = exact_dot(full[:ROWS, 2 * HD:], out_weight)
        maps_out[step, :ROWS, :] = jnp.concatenate([score_map, value_map], axis=1).astype(BF16)
        maps_out[step, ROWS:, :] = other_columns.astype(BF16)
        maps_in[step, head, :MAP_ROWS, :] = maps_out[step]

    def send_maps(step):
        got_maps.append(
            send_plane(
                2 + step,
                lambda peer: maps_out.at[step],
                lambda slot: maps_in.at[step, slot, pl.ds(0, MAP_ROWS)],
            )
        )

    make_maps(0)
    send_maps(0)
    make_maps(1)
    send_maps(1)

    def first_lanes(features):
        lane = lax.broadcasted_iota(jnp.int32, features.shape, 1)
        return jnp.where(lane < KEY, features, jnp.zeros_like(features))

    def mapped(features, step, slots):
        features = first_lanes(features)
        lane = lax.broadcasted_iota(jnp.int32, features.shape, 1)
        result = []
        for slot in slots:
            maps = maps_in[step, slot]
            columns, others = dot(features, maps), dot(features, maps, NT)
            result.append(jnp.where(lane < QUERY, columns, jnp.where(lane < KEY, 0.0, others)))
        return jnp.concatenate(result, axis=0).astype(BF16)

    def attend(queries, keys, step, slots):
        count = queries.shape[0] // len(slots)
        exponent = jnp.exp2(dot(queries, keys, NT))
        weights = exponent * (1.0 / jnp.sum(exponent, axis=-1, keepdims=True))
        attended = first_lanes(dot(weights.astype(BF16), keys)).astype(BF16)
        sides = jnp.concatenate(
            [attended[i * count:(i + 1) * count] for i in range(len(slots))], axis=1
        )
        return dot(sides, jnp.concatenate([maps_in[step, slot] for slot in slots], axis=0))

    near_first = ((0, 0),) + OFFSETS[::-1]

    arrived(("plane", 1))
    keys = tokens[0].reshape(heads * both, 128)
    features = tokens[0, head]
    arriving.pop(("plane", 2))
    velocity = jnp.zeros((both, 128), F32)
    for i in range(0, heads, 4):
        offsets = near_first[i:i + 4]
        got_maps[0](offsets[1:] if i == 0 else offsets)
        slots = [peer_at(offset) for offset in offsets]
        velocity += attend(mapped(features, 0, slots), keys, 0, slots)
    arrived("carry")
    carry_rows = jnp.concatenate([unpack(carry[i]) for i in range(2)], axis=0)
    state[...] = carry_rows + added(velocity[:, C:], start)
    tokens[1, head] = token_features(state[...].astype(BF16), in_weight_bf, in_bias)
    send_plane(4, lambda peer: tokens.at[1, head], lambda slot: tokens.at[1, slot])
    arrived(("plane", 3))
    slots = [peer_at(offset) for offset in near_first]
    queries = mapped(tokens[1, head, own_rows, :], 1, slots)
    arrived(("plane", 4))

    keys = tokens[1].reshape(heads * both, 128)
    velocity = jnp.zeros((own, 128), F32)
    for i in range(0, heads, 8):
        velocity += attend(queries[i * own:(i + 8) * own], keys, 1, slots[i:i + 8])
    velocity = velocity[:, C:]
    loads["noise1"].wait()
    latent = carried(state[own_rows, :], noise1[...], start + 1) + added(velocity, start + 1)
    result[0] = jnp.concatenate([latent, velocity], axis=1)

    for name in list(leaving):
        left(name)


def shards(groups, heads):
    def run(
        latent, step_noise, start_index, mod_table, in_weight, in_bias,
        base_weight, factor_store, block_order, out_weight,
    ):
        own = latent.shape[1]
        block_rows = (factor_store.shape[0] + 15) // 16 * 16
        total = (D // 128 + heads) * 16
        vmem = pl.BlockSpec(memory_space=pltpu.VMEM)
        anywhere = pl.BlockSpec(memory_space=pl.ANY)
        result = pl.pallas_call(
            functools.partial(kernel, groups, heads),
            out_shape=jax.ShapeDtypeStruct((1, own, 2 * C), F32),
            in_specs=[
                pl.BlockSpec(memory_space=pltpu.SMEM),
                *[anywhere] * 9,
            ],
            out_specs=vmem,
            scratch_shapes=[
                pltpu.VMEM(mod_table.shape, F32),
                pltpu.VMEM(in_weight.shape, BF16),
                pltpu.VMEM((1, D), F32),
                pltpu.VMEM(base_weight.shape, BF16),
                pltpu.VMEM(factor_store.shape, BF16),
                pltpu.VMEM((1, block_order.shape[0]), jnp.int32),
                pltpu.VMEM((own, C), F32),
                pltpu.VMEM((own, C), F32),
                pltpu.VMEM((own, C), F32),
                pltpu.VMEM(out_weight.shape, BF16),
                pltpu.VMEM((2, own // 2 + 32, 128), BF16),
                pltpu.VMEM((2, own // 2, 128), F32),
                pltpu.VMEM((2 * own, C), F32),
                pltpu.VMEM((2, groups // 2, block_rows, 256), BF16),
                pltpu.VMEM((total, 256), BF16),
                pltpu.VMEM((total, 256), BF16),
                pltpu.VMEM((STEPS, 128, D), BF16),
                pltpu.VMEM((STEPS, 128, 3 * HD), F32),
                pltpu.VMEM((STEPS, 3 * QUERY + 16, HD), BF16),
                pltpu.VMEM((STEPS, 3 * QUERY + 16, HD), BF16),
                pltpu.VMEM((heads, 16, 384), BF16),
                pltpu.VMEM((heads, 16, 384), BF16),
                pltpu.VMEM((STEPS, heads, 2 * own, 128), BF16),
                pltpu.VMEM((STEPS, MAP_ROWS, 128), BF16),
                pltpu.VMEM((STEPS, heads, 128, 128), BF16),
                pltpu.SemaphoreType.DMA((10,)),
                pltpu.SemaphoreType.DMA((groups // 2,)),
                pltpu.SemaphoreType.DMA((groups // 2,)),
                pltpu.SemaphoreType.DMA((5,)),
                pltpu.SemaphoreType.DMA((5,)),
                pltpu.SemaphoreType.DMA((5, heads)),
                pltpu.SemaphoreType.DMA((5, heads)),
                pltpu.SemaphoreType.REGULAR,
                pltpu.SemaphoreType.REGULAR,
            ],
            compiler_params=pltpu.CompilerParams(
                collective_id=0, has_side_effects=True, vmem_limit_bytes=63 * 1024 * 1024
            ),
        )(
            start_index, latent, step_noise, mod_table, in_weight, in_bias.reshape(1, -1),
            base_weight, factor_store, block_order.reshape(1, -1), out_weight,
        )
        return result[:, :, :C], result[:, :, C:]

    return run


def solution(mesh):
    in_specs = (
        P("grp", "seq", None),
        P("grp", None, "seq", None),
        P("grp"),
        P(),
        P(),
        P(),
        P(None, "seq", None, None),
        P("grp", None),
        P(),
        P("seq", None),
    )
    out_specs = (P("grp", "seq", None), P("grp", "seq", None))
    run = shards(mesh.shape["grp"], mesh.shape["seq"] // 2)
    return jax.shard_map(run, mesh=mesh, in_specs=in_specs, out_specs=out_specs, check_vma=False)
```

```python
import functools
import math

import jax
import jax.numpy as jnp
from jax import lax
from jax.experimental import pallas as pl
from jax.experimental.pallas import tpu as pltpu
from jax.sharding import PartitionSpec as P

D = 3072
C = 64
HD = 128
RANK = 64
BW = 64
TSTEPS = 10
STEPS = 2
MESH = pl.DeviceIdType.MESH
F32 = jnp.float32
BF16 = jnp.bfloat16
QUERY = 64
KEY = 80
ROWS = 80
MAP_ROWS = 96
NT = (((1,), (1,)), ((), ()))
SIDE = 4
OFFSETS = (
    (2, 2), (2, 1), (2, 3), (1, 2), (3, 2), (1, 1), (3, 3), (1, 3), (3, 1),
    (2, 0), (0, 2), (1, 0), (3, 0), (0, 1), (0, 3),
)


def dot(a, b, dims=(((1,), (0,)), ((), ()))):
    return lax.dot_general(a, b, dims, preferred_element_type=F32)


def exact_dot(a, b, dims=(((1,), (0,)), ((), ()))):
    return lax.dot_general(
        a, b, dims, preferred_element_type=F32, precision=lax.Precision.HIGHEST
    )


def sigma_at(index):
    remaining = 1.0 - index.astype(F32) / TSTEPS
    return 3.0 * remaining / (1.0 + 2.0 * remaining)


def plan(index):
    sigma_now = sigma_at(index)
    sigma_step = sigma_at(index + 1) - sigma_now
    spread = 0.7 * jnp.sqrt(sigma_now / (1.0 - sigma_now))
    return (sigma_now, sigma_step, spread)


def carried(state, noise, index):
    sigma_now, sigma_step, spread = plan(jnp.full(state.shape, index, jnp.int32))
    return (
        state * (1.0 + spread * spread / (2.0 * sigma_now) * sigma_step)
        + spread * jnp.sqrt(-sigma_step) * noise
    )


def added(velocity, index):
    sigma_now, sigma_step, spread = plan(jnp.full(velocity.shape, index, jnp.int32))
    return velocity * (1.0 + spread * spread * (1.0 - sigma_now) / (2.0 * sigma_now)) * sigma_step


def pack(rows):
    count = rows.shape[0] // 2
    return jnp.concatenate([rows[:count], rows[count:]], axis=1)


def unpack(rows):
    return jnp.concatenate([rows[:, :64], rows[:, 64:]], axis=0)


def token_features(latent_in, in_weight, in_bias):
    hidden = dot(latent_in, in_weight) + in_bias
    average = jnp.mean(hidden, axis=-1, keepdims=True)
    centred = hidden - average
    variance = jnp.mean(centred * centred, axis=-1, keepdims=True)
    scale = lax.rsqrt(variance + 1e-06)
    scaled = latent_in.astype(F32) * scale
    high = scale.astype(BF16).astype(F32)
    lane = lax.broadcasted_iota(jnp.int32, scaled.shape, 1)
    entry = jnp.where(lane < 2 * (KEY - QUERY), lane & (KEY - QUERY - 1), 3)
    rest = jnp.where(
        entry == 0, high, jnp.where(entry == 1, 1.0, jnp.where(entry == 2, scale - high, 0.0))
    )
    return jnp.concatenate([scaled, rest], axis=1).astype(BF16)


def kernel(
    groups, heads,
    start_ref, latent_hbm, noise_hbm, mod_hbm, win_hbm, bias_hbm, base_hbm, fac_hbm, order_hbm, wout_hbm,
    result,
    mod, win, bias_ref, base, fac_ref, order_ref, latent0, noise0, noise1, wout_half,
    hello, carry, state, store, perm_even, perm_odd, folded,
    own_part, part_out, part_in, rank_out, rank_in, tokens, maps_out, maps_in,
    load_sem, col_send, col_recv, pair_send, pair_recv, plane_send, plane_recv, ready, heard,
):
    g = lax.axis_index("grp")
    s = lax.axis_index("seq")
    core, zlo = g % 2, g // 2
    zcount = groups // 2
    head, half = s // 2, s % 2
    own = latent_hbm.shape[1]
    both = 2 * own
    half_d = D // 2
    store_rows = fac_hbm.shape[0]
    block_rows = store.shape[2]
    pairs = D // 128
    per_member = 2 * (pairs + heads)

    sibling = (g + 1 - 2 * core, s)
    partner = (g, s + 1 - 2 * half)

    def column_target(j):
        return jnp.where(zlo < zcount // 2, zcount - 1 - j, j)

    def column(other):
        return (other * 2 + core, s)

    def peer_at(offset):
        dx, dy = offset
        return (head // SIDE + dx) % SIDE * SIDE + (head % SIDE + dy) % SIDE

    def plane(h):
        return (g, h * 2 + half)

    loads = {
        name: pltpu.make_async_copy(src, dst, load_sem.at[i])
        for i, (name, src, dst) in enumerate(
            [
                ("factors", fac_hbm, fac_ref),
                ("in_weight", win_hbm, win),
                ("table", mod_hbm, mod),
                ("in_bias", bias_hbm, bias_ref),
                ("base", base_hbm, base),
                ("latent", latent_hbm.at[0], latent0),
                ("noise0", noise_hbm.at[0, 0], noise0),
                ("out_weight", wout_hbm, wout_half),
                ("order", order_hbm, order_ref),
                ("noise1", noise_hbm.at[0, 1], noise1),
            ]
        )
    }
    loads["factors"].start()

    barrier = pltpu.get_barrier_semaphore()

    def greet(device):
        pl.semaphore_signal(barrier, inc=1, device_id=device, device_id_type=MESH)

    @pl.when(half == 0)
    def _():
        greet((zlo * 2, s + 1))

    for j in range(zcount):
        other = column_target(j)

        @pl.when(other != zlo)
        def _():
            greet((other * 2 + half, s))

    for offset in OFFSETS:
        greet((zlo * 2 + 1, peer_at(offset) * 2 + half))
    greet(sibling)
    in_columns, in_planes = 2 * (zcount - 1), 2 * (heads - 1)

    for name in list(loads)[1:]:
        loads[name].start()

    arriving, leaving = {}, {}

    def column_copy(slot, other):
        place = store.at[core, slot]
        return pltpu.make_async_remote_copy(
            src_ref=place, dst_ref=place,
            send_sem=col_send.at[other], recv_sem=col_recv.at[slot],
            device_id=column(other), device_id_type=MESH,
        )

    def each_column(action):
        for j in range(zcount):
            other = column_target(j)

            @pl.when(other != zlo)
            def _():
                action(other)

    @pl.when(core == 0)
    def _():
        pl.semaphore_wait(barrier, 1 + jnp.where(half == 0, in_columns, 2))
        pl.semaphore_signal(heard, inc=1, device_id=sibling, device_id_type=MESH)

    @pl.when(core == 1)
    def _():
        pl.semaphore_wait(heard, 1)

    @pl.when(half == 1)
    def _():
        pl.semaphore_signal(ready, inc=1, device_id=partner, device_id_type=MESH)

    loads["factors"].wait()
    store[core, zlo] = jnp.zeros(store.shape[2:], BF16)
    lanes = pl.ds(pl.multiple_of(head * 256, 256), 256)
    store[core, zlo, :store_rows, :] = fac_ref[:, lanes]

    @pl.when(half == 0)
    def _():
        each_column(lambda other: column_copy(zlo, other).start())

    start = start_ref[0]
    for name in ("in_weight", "in_bias", "table"):
        loads[name].wait()
    in_weight = win[...].astype(F32)
    in_bias = bias_ref[...]
    weight_centred = in_weight - jnp.mean(in_weight, axis=-1, keepdims=True)
    bias_centred = in_bias - jnp.mean(in_bias, axis=-1, keepdims=True)
    extra_row = lax.broadcasted_iota(jnp.int32, (16, D), 0)
    for step in range(STEPS):
        shift = mod[pl.ds(start + step, 1), :D]
        gain = 1.0 + mod[pl.ds(start + step, 1), D:]
        folded[step, :64, :] = (weight_centred * gain).astype(BF16)
        is_bias = (extra_row == 0) | (extra_row == 2)
        extra = jnp.where(is_bias, bias_centred * gain, jnp.where(extra_row == 1, shift, 0.0))
        folded[step, 64:80, :] = extra.astype(BF16)
        folded[step, 80:, :] = jnp.zeros((48, D), BF16)

    loads["base"].wait()
    half_lanes = pl.ds(pl.multiple_of(half * half_d, 128), half_d)
    extras = [[None] * 3 for _ in range(STEPS)]
    for member in range(3):
        part = dot(folded[:, :, half_lanes].reshape(STEPS * 128, half_d), base[member, 0])
        for step in range(STEPS):
            piece = part[step * 128:(step + 1) * 128]
            own_part[step, :, member * HD:(member + 1) * HD] = piece
            part_out[step, member * QUERY:(member + 1) * QUERY, :] = piece[:QUERY].astype(BF16)
            extras[step][member] = piece[QUERY:QUERY + 2]
    for step in range(STEPS):
        rest = jnp.concatenate(extras[step] + [jnp.zeros((10, HD), F32)], axis=0)
        part_out[step, 3 * QUERY:, :] = rest.astype(BF16)

    for name in ("latent", "noise0", "out_weight"):
        loads[name].wait()
    hello[half, :own // 2, :] = pack(latent0[...]).astype(BF16)
    hello[half, own // 2:, :] = pack(wout_half[...].astype(F32)).astype(BF16)
    carry[half] = pack(carried(latent0[...], noise0[...], start))
    own_rows = pl.ds(pl.multiple_of(half * own, own), own)
    for step in range(STEPS):
        maps_in[step, :, MAP_ROWS:, :] = jnp.zeros((heads, 128 - MAP_ROWS, 128), BF16)

    def arrived(name):
        arriving.pop(name)()

    def left(name):
        leaving.pop(name)()

    def pair_copy(i, src, dst, device=partner):
        return pltpu.make_async_remote_copy(
            src_ref=src, dst_ref=dst,
            send_sem=pair_send.at[i], recv_sem=pair_recv.at[i],
            device_id=device, device_id_type=MESH,
        )

    def exchange(name, i, out, into, device=partner):
        copy = pair_copy(i, out, out, device)
        copy.start()
        arriving[name] = pair_copy(i, into, into, device).wait_recv
        leaving[name] = copy.wait_send

    hello_copy = pair_copy(0, hello.at[half], hello.at[half])
    carry_copy = pair_copy(1, carry.at[half], carry.at[half])
    part_copies = [pair_copy(3 + step, part_out.at[step], part_in.at[step]) for step in range(STEPS)]

    def start_pair():
        part_copies[0].start()

    def start_late_pair():
        carry_copy.start()
        part_copies[1].start()

    @pl.when(half == 1)
    def _():
        hello_copy.start()

    @pl.when(core == 1)
    def _():
        pl.semaphore_wait(barrier, 1 + in_planes + jnp.where(half == 0, 0, in_columns))
        pl.semaphore_signal(heard, inc=1, device_id=sibling, device_id_type=MESH)

    @pl.when(core == 0)
    def _():
        pl.semaphore_wait(heard, 1)

    @pl.when(half == 1)
    def _():
        each_column(lambda other: column_copy(zlo, other).start())
        start_pair()

    arriving["column"] = lambda: each_column(lambda other: column_copy(other, other).wait_recv())
    leaving["column"] = lambda: each_column(lambda other: column_copy(zlo, other).wait_send())

    def plane_copy(kind, src, dst, peer, slot):
        return pltpu.make_async_remote_copy(
            src_ref=src, dst_ref=dst,
            send_sem=plane_send.at[kind, peer], recv_sem=plane_recv.at[kind, slot],
            device_id=plane(peer), device_id_type=MESH,
        )

    def send_plane(kind, src_of, place_of):
        def receive(offsets=OFFSETS):
            for offset in offsets:
                peer = peer_at(offset)
                plane_copy(kind, src_of(peer), place_of(peer), peer, peer).wait_recv()

        def finish():
            for offset in OFFSETS:
                peer = peer_at(offset)
                plane_copy(kind, src_of(peer), place_of(head), peer, head).wait_send()

        for offset in OFFSETS:
            peer = peer_at(offset)
            plane_copy(kind, src_of(peer), place_of(head), peer, head).start()
        arriving["plane", kind] = receive
        leaving["plane", kind] = finish
        return receive

    stored = zcount * 2 * store_rows
    row = lax.broadcasted_iota(jnp.int32, (stored, 256), 0)
    col = lax.broadcasted_iota(jnp.int32, (stored, 256), 1)
    in_block = col % block_rows
    slot = col // block_rows
    shard = slot % zcount * 2 + slot // zcount
    source = jnp.where(in_block < store_rows, shard * store_rows + in_block, -1)
    place = (row == source).astype(F32).astype(BF16)
    loads["order"].wait()
    order = jnp.broadcast_to((order_ref[...] + 1).astype(F32), (16, stored)).astype(BF16)
    order = dot(order, place)[0:1].astype(jnp.int32) - 1
    total = (pairs + heads) * 16
    line = lax.broadcasted_iota(jnp.int32, (total, 256), 0)
    entry = line & 15
    member_of = entry - 3 * ((entry * 11) >> 5)
    target = jnp.where(entry < 12, member_of * per_member + 2 * (line >> 4), -8)
    perm_even[...] = (target == order).astype(F32).astype(BF16)
    perm_odd[...] = (target + 1 == order).astype(F32).astype(BF16)

    arrived("column")
    exchange("sibling", 2, store.at[core], store.at[1 - core], sibling)

    @pl.when(half == 0)
    def _():
        pl.semaphore_wait(ready, 1)
        hello_copy.start()
        start_pair()

    @pl.when(half == 1)
    def _():
        start_late_pair()

    arrived("sibling")
    blocks = store[...].reshape(256, 256)
    even = dot(perm_even[...], blocks)
    odd = dot(perm_odd[...], blocks)
    lane = lax.broadcasted_iota(jnp.int32, (total, 128), 1)
    entry = lax.broadcasted_iota(jnp.int32, (total, 128), 0) & 15
    rank = (entry * 11) >> 5
    even = jnp.where(rank < 2, even[:, :128], even[:, 128:])
    odd = jnp.where(rank < 2, odd[:, :128], odd[:, 128:])
    first = (rank & 1) == 0
    spread = jnp.where(
        lane < 64,
        jnp.where(first, even, pltpu.roll(even, 64, 1)),
        jnp.where(first, pltpu.roll(odd, 64, 1), odd),
    ).astype(BF16)
    lower = jnp.concatenate([spread[i * 16:(i + 1) * 16] for i in range(pairs)], axis=1)
    inner = [dot(lower, folded[step], NT).astype(BF16) for step in range(STEPS)]
    for other in range(heads):
        rank_out[other, :, 0:128] = inner[0]
        rank_out[other, :, 128:256] = inner[1]
        rank_out[other, :, 256:384] = spread[(pairs + other) * 16:(pairs + other + 1) * 16]
    rank_in[head] = rank_out[head]
    send_plane(0, lambda peer: rank_out.at[peer], lambda slot: rank_in.at[slot])

    for name, i, buffer, copy in (("hello", 0, hello, hello_copy), ("carry", 1, carry, carry_copy)):
        arriving[name] = pair_copy(i, buffer.at[1 - half], buffer.at[1 - half]).wait_recv
        leaving[name] = copy.wait_send
    for step in range(STEPS):
        arriving["part", step] = part_copies[step].wait_recv
        leaving["part", step] = part_copies[step].wait_send

    arrived("hello")
    in_weight_bf = win[...]
    latent_in = jnp.concatenate(
        [unpack(hello[i, :own // 2, :].astype(F32)) for i in range(2)], axis=0
    ).astype(BF16)
    tokens[0, head] = token_features(latent_in, in_weight_bf, in_bias)
    send_plane(1, lambda peer: tokens.at[0, head], lambda slot: tokens.at[0, slot])

    arrived(("plane", 0))
    ranks = rank_in[...].reshape(heads * 16, 384)
    entry = lax.broadcasted_iota(jnp.int32, (heads * 16, HD), 0) & 15
    member_of = entry - 3 * ((entry * 11) >> 5)
    upper = ranks[:, 256:].astype(F32)
    upper = jnp.concatenate(
        [jnp.where(member_of == member, upper, 0.0) for member in range(3)], axis=1
    ).astype(BF16)
    low_rank = dot(ranks[:, :256].astype(F32).T.astype(BF16), upper)
    out_weight = jnp.concatenate(
        [unpack(hello[i, own // 2:, :].astype(F32)) for i in range(2)], axis=0
    )
    got_maps = []

    def make_maps(step):
        arrived(("part", step))
        received = part_in[step].astype(F32)
        rest = received[3 * QUERY:]
        received = jnp.concatenate(
            [
                jnp.concatenate(
                    [
                        received[member * QUERY:(member + 1) * QUERY],
                        rest[2 * member:2 * member + 2],
                        rest[2 * member:2 * member + 1],
                        jnp.zeros((128 - QUERY - 3, HD), F32),
                    ],
                    axis=0,
                )
                for member in range(3)
            ],
            axis=1,
        )
        full = own_part[step] + received + low_rank[step * 128:(step + 1) * 128]
        to_score = HD ** (-0.5) * math.log2(math.e)
        queries, keys = full[:, :HD] * to_score, full[:, HD:2 * HD]
        score_map = exact_dot(queries[:ROWS], keys[:QUERY], NT)
        other_columns = exact_dot(keys[QUERY:ROWS], queries, NT)
        value_map = exact_dot(full[:ROWS, 2 * HD:], out_weight)
        maps_out[step, :ROWS, :] = jnp.concatenate([score_map, value_map], axis=1).astype(BF16)
        maps_out[step, ROWS:, :] = other_columns.astype(BF16)
        maps_in[step, head, :MAP_ROWS, :] = maps_out[step]

    def send_maps(step):
        got_maps.append(
            send_plane(
                2 + step,
                lambda peer: maps_out.at[step],
                lambda slot: maps_in.at[step, slot, pl.ds(0, MAP_ROWS)],
            )
        )

    make_maps(0)
    send_maps(0)

    @pl.when(half == 0)
    def _():
        start_late_pair()

    make_maps(1)
    send_maps(1)

    def first_lanes(features):
        lane = lax.broadcasted_iota(jnp.int32, features.shape, 1)
        return jnp.where(lane < KEY, features, jnp.zeros_like(features))

    def mapped(features, step, slots):
        features = first_lanes(features)
        lane = lax.broadcasted_iota(jnp.int32, features.shape, 1)
        result = []
        for slot in slots:
            maps = maps_in[step, slot]
            columns, others = dot(features, maps), dot(features, maps, NT)
            result.append(jnp.where(lane < QUERY, columns, jnp.where(lane < KEY, 0.0, others)))
        return jnp.concatenate(result, axis=0).astype(BF16)

    def attend(queries, keys, step, slots):
        count = queries.shape[0] // len(slots)
        exponent = jnp.exp2(dot(queries, keys, NT))
        weights = exponent * (1.0 / jnp.sum(exponent, axis=-1, keepdims=True))
        attended = first_lanes(dot(weights.astype(BF16), keys)).astype(BF16)
        sides = jnp.concatenate(
            [attended[i * count:(i + 1) * count] for i in range(len(slots))], axis=1
        )
        return dot(sides, jnp.concatenate([maps_in[step, slot] for slot in slots], axis=0))

    near_first = ((0, 0),) + OFFSETS[::-1]

    arrived(("plane", 1))
    keys = tokens[0].reshape(heads * both, 128)
    features = tokens[0, head]
    arriving.pop(("plane", 2))
    velocity = jnp.zeros((both, 128), F32)
    for i in range(0, heads, 4):
        offsets = near_first[i:i + 4]
        got_maps[0](offsets[1:] if i == 0 else offsets)
        slots = [peer_at(offset) for offset in offsets]
        velocity += attend(mapped(features, 0, slots), keys, 0, slots)
    arrived("carry")
    carry_rows = jnp.concatenate([unpack(carry[i]) for i in range(2)], axis=0)
    state[...] = carry_rows + added(velocity[:, C:], start)
    tokens[1, head] = token_features(state[...].astype(BF16), in_weight_bf, in_bias)
    send_plane(4, lambda peer: tokens.at[1, head], lambda slot: tokens.at[1, slot])
    arrived(("plane", 3))
    slots = [peer_at(offset) for offset in near_first]
    queries = mapped(tokens[1, head, own_rows, :], 1, slots)
    arrived(("plane", 4))

    keys = tokens[1].reshape(heads * both, 128)
    velocity = jnp.zeros((own, 128), F32)
    for i in range(0, heads, 8):
        velocity += attend(queries[i * own:(i + 8) * own], keys, 1, slots[i:i + 8])
    velocity = velocity[:, C:]
    loads["noise1"].wait()
    latent = carried(state[own_rows, :], noise1[...], start + 1) + added(velocity, start + 1)
    result[0] = jnp.concatenate([latent, velocity], axis=1)

    for name in list(leaving):
        left(name)


def shards(groups, heads):
    def run(
        latent, step_noise, start_index, mod_table, in_weight, in_bias,
        base_weight, factor_store, block_order, out_weight,
    ):
        own = latent.shape[1]
        block_rows = (factor_store.shape[0] + 15) // 16 * 16
        total = (D // 128 + heads) * 16
        vmem = pl.BlockSpec(memory_space=pltpu.VMEM)
        anywhere = pl.BlockSpec(memory_space=pl.ANY)
        result = pl.pallas_call(
            functools.partial(kernel, groups, heads),
            out_shape=jax.ShapeDtypeStruct((1, own, 2 * C), F32),
            in_specs=[
                pl.BlockSpec(memory_space=pltpu.SMEM),
                *[anywhere] * 9,
            ],
            out_specs=vmem,
            scratch_shapes=[
                pltpu.VMEM(mod_table.shape, F32),
                pltpu.VMEM(in_weight.shape, BF16),
                pltpu.VMEM((1, D), F32),
                pltpu.VMEM(base_weight.shape, BF16),
                pltpu.VMEM(factor_store.shape, BF16),
                pltpu.VMEM((1, block_order.shape[0]), jnp.int32),
                pltpu.VMEM((own, C), F32),
                pltpu.VMEM((own, C), F32),
                pltpu.VMEM((own, C), F32),
                pltpu.VMEM(out_weight.shape, BF16),
                pltpu.VMEM((2, own // 2 + 32, 128), BF16),
                pltpu.VMEM((2, own // 2, 128), F32),
                pltpu.VMEM((2 * own, C), F32),
                pltpu.VMEM((2, groups // 2, block_rows, 256), BF16),
                pltpu.VMEM((total, 256), BF16),
                pltpu.VMEM((total, 256), BF16),
                pltpu.VMEM((STEPS, 128, D), BF16),
                pltpu.VMEM((STEPS, 128, 3 * HD), F32),
                pltpu.VMEM((STEPS, 3 * QUERY + 16, HD), BF16),
                pltpu.VMEM((STEPS, 3 * QUERY + 16, HD), BF16),
                pltpu.VMEM((heads, 16, 384), BF16),
                pltpu.VMEM((heads, 16, 384), BF16),
                pltpu.VMEM((STEPS, heads, 2 * own, 128), BF16),
                pltpu.VMEM((STEPS, MAP_ROWS, 128), BF16),
                pltpu.VMEM((STEPS, heads, 128, 128), BF16),
                pltpu.SemaphoreType.DMA((10,)),
                pltpu.SemaphoreType.DMA((groups // 2,)),
                pltpu.SemaphoreType.DMA((groups // 2,)),
                pltpu.SemaphoreType.DMA((5,)),
                pltpu.SemaphoreType.DMA((5,)),
                pltpu.SemaphoreType.DMA((5, heads)),
                pltpu.SemaphoreType.DMA((5, heads)),
                pltpu.SemaphoreType.REGULAR,
                pltpu.SemaphoreType.REGULAR,
            ],
            compiler_params=pltpu.CompilerParams(
                collective_id=0, has_side_effects=True, vmem_limit_bytes=63 * 1024 * 1024
            ),
        )(
            start_index, latent, step_noise, mod_table, in_weight, in_bias.reshape(1, -1),
            base_weight, factor_store, block_order.reshape(1, -1), out_weight,
        )
        return result[:, :, :C], result[:, :, C:]

    return run


def solution(mesh):
    in_specs = (
        P("grp", "seq", None),
        P("grp", None, "seq", None),
        P("grp"),
        P(),
        P(),
        P(),
        P(None, "seq", None, None),
        P("grp", None),
        P(),
        P("seq", None),
    )
    out_specs = (P("grp", "seq", None), P("grp", "seq", None))
    run = shards(mesh.shape["grp"], mesh.shape["seq"] // 2)
    return jax.shard_map(run, mesh=mesh, in_specs=in_specs, out_specs=out_specs, check_vma=False)
```

```python
import functools
import math

import jax
import jax.numpy as jnp
from jax import lax
from jax.experimental import pallas as pl
from jax.experimental.pallas import tpu as pltpu
from jax.sharding import PartitionSpec as P

D = 3072
C = 64
HD = 128
RANK = 64
BW = 64
TSTEPS = 10
STEPS = 2
MESH = pl.DeviceIdType.MESH
F32 = jnp.float32
BF16 = jnp.bfloat16
QUERY = 64
KEY = 80
ROWS = 80
MAP_ROWS = 96
NT = (((1,), (1,)), ((), ()))
SIDE = 4
OFFSETS = (
    (2, 2), (2, 1), (2, 3), (1, 2), (3, 2), (1, 1), (3, 3), (1, 3), (3, 1),
    (2, 0), (0, 2), (1, 0), (3, 0), (0, 1), (0, 3),
)


def dot(a, b, dims=(((1,), (0,)), ((), ()))):
    return lax.dot_general(a, b, dims, preferred_element_type=F32)


def exact_dot(a, b, dims=(((1,), (0,)), ((), ()))):
    return lax.dot_general(
        a, b, dims, preferred_element_type=F32, precision=lax.Precision.HIGHEST
    )


def sigma_at(index):
    remaining = 1.0 - index.astype(F32) / TSTEPS
    return 3.0 * remaining / (1.0 + 2.0 * remaining)


def plan(index):
    sigma_now = sigma_at(index)
    sigma_step = sigma_at(index + 1) - sigma_now
    spread = 0.7 * jnp.sqrt(sigma_now / (1.0 - sigma_now))
    return (sigma_now, sigma_step, spread)


def carried(state, noise, index):
    sigma_now, sigma_step, spread = plan(jnp.full(state.shape, index, jnp.int32))
    return (
        state * (1.0 + spread * spread / (2.0 * sigma_now) * sigma_step)
        + spread * jnp.sqrt(-sigma_step) * noise
    )


def added(velocity, index):
    sigma_now, sigma_step, spread = plan(jnp.full(velocity.shape, index, jnp.int32))
    return velocity * (1.0 + spread * spread * (1.0 - sigma_now) / (2.0 * sigma_now)) * sigma_step


def pack(rows):
    count = rows.shape[0] // 2
    return jnp.concatenate([rows[:count], rows[count:]], axis=1)


def unpack(rows):
    return jnp.concatenate([rows[:, :64], rows[:, 64:]], axis=0)


def token_features(latent_in, in_weight, in_bias):
    hidden = dot(latent_in, in_weight) + in_bias
    average = jnp.mean(hidden, axis=-1, keepdims=True)
    centred = hidden - average
    variance = jnp.mean(centred * centred, axis=-1, keepdims=True)
    scale = lax.rsqrt(variance + 1e-06)
    scaled = latent_in.astype(F32) * scale
    high = scale.astype(BF16).astype(F32)
    lane = lax.broadcasted_iota(jnp.int32, scaled.shape, 1)
    entry = jnp.where(lane < 2 * (KEY - QUERY), lane & (KEY - QUERY - 1), 3)
    rest = jnp.where(
        entry == 0, high, jnp.where(entry == 1, 1.0, jnp.where(entry == 2, scale - high, 0.0))
    )
    return jnp.concatenate([scaled, rest], axis=1).astype(BF16)


def kernel(
    groups, heads,
    start_ref, latent_hbm, noise_hbm, mod_hbm, win_hbm, bias_hbm, base_hbm, fac_hbm, order_hbm, wout_hbm,
    result,
    mod, win, bias_ref, base, fac_ref, order_ref, latent0, noise0, noise1, wout_half,
    hello, carry, state, store, perm_even, perm_odd, folded,
    own_part, part_out, part_in, rank_out, rank_in, tokens, maps_out, maps_in,
    load_sem, col_send, col_recv, pair_send, pair_recv, plane_send, plane_recv, ready, heard,
):
    g = lax.axis_index("grp")
    s = lax.axis_index("seq")
    core, zlo = g % 2, g // 2
    zcount = groups // 2
    head, half = s // 2, s % 2
    own = latent_hbm.shape[1]
    both = 2 * own
    half_d = D // 2
    store_rows = fac_hbm.shape[0]
    block_rows = store.shape[2]
    pairs = D // 128
    per_member = 2 * (pairs + heads)

    sibling = (g + 1 - 2 * core, s)
    partner = (g, s + 1 - 2 * half)

    def column_target(j):
        return jnp.where(zlo < zcount // 2, zcount - 1 - j, j)

    def column(other):
        return (other * 2 + core, s)

    def peer_at(offset):
        dx, dy = offset
        return (head // SIDE + dx) % SIDE * SIDE + (head % SIDE + dy) % SIDE

    def plane(h):
        return (g, h * 2 + half)

    loads = {
        name: pltpu.make_async_copy(src, dst, load_sem.at[i])
        for i, (name, src, dst) in enumerate(
            [
                ("factors", fac_hbm, fac_ref),
                ("in_weight", win_hbm, win),
                ("table", mod_hbm, mod),
                ("in_bias", bias_hbm, bias_ref),
                ("base", base_hbm, base),
                ("latent", latent_hbm.at[0], latent0),
                ("noise0", noise_hbm.at[0, 0], noise0),
                ("out_weight", wout_hbm, wout_half),
                ("order", order_hbm, order_ref),
                ("noise1", noise_hbm.at[0, 1], noise1),
            ]
        )
    }
    loads["factors"].start()

    barrier = pltpu.get_barrier_semaphore()

    def greet(device):
        pl.semaphore_signal(barrier, inc=1, device_id=device, device_id_type=MESH)

    @pl.when(half == 0)
    def _():
        greet((zlo * 2, s + 1))

    for j in range(zcount):
        other = column_target(j)

        @pl.when(other != zlo)
        def _():
            greet((other * 2 + half, s))

    for offset in OFFSETS:
        greet((zlo * 2 + 1, peer_at(offset) * 2 + half))
    greet(sibling)
    in_columns, in_planes = 2 * (zcount - 1), 2 * (heads - 1)

    for name in list(loads)[1:]:
        loads[name].start()

    arriving, leaving = {}, {}

    def column_copy(slot, other):
        place = store.at[core, slot]
        return pltpu.make_async_remote_copy(
            src_ref=place, dst_ref=place,
            send_sem=col_send.at[other], recv_sem=col_recv.at[slot],
            device_id=column(other), device_id_type=MESH,
        )

    def each_column(action):
        for j in range(zcount):
            other = column_target(j)

            @pl.when(other != zlo)
            def _():
                action(other)

    @pl.when(core == 0)
    def _():
        pl.semaphore_wait(barrier, 1 + jnp.where(half == 0, in_columns, 2))
        pl.semaphore_signal(heard, inc=1, device_id=sibling, device_id_type=MESH)

    @pl.when(core == 1)
    def _():
        pl.semaphore_wait(heard, 1)

    @pl.when(half == 1)
    def _():
        pl.semaphore_signal(ready, inc=1, device_id=partner, device_id_type=MESH)

    loads["factors"].wait()
    store[core, zlo] = jnp.zeros(store.shape[2:], BF16)
    lanes = pl.ds(pl.multiple_of(head * 256, 256), 256)
    store[core, zlo, :store_rows, :] = fac_ref[:, lanes]

    @pl.when(half == 0)
    def _():
        each_column(lambda other: column_copy(zlo, other).start())

    start = start_ref[0]
    for name in ("in_weight", "in_bias", "table"):
        loads[name].wait()
    in_weight = win[...].astype(F32)
    in_bias = bias_ref[...]
    weight_centred = in_weight - jnp.mean(in_weight, axis=-1, keepdims=True)
    bias_centred = in_bias - jnp.mean(in_bias, axis=-1, keepdims=True)
    extra_row = lax.broadcasted_iota(jnp.int32, (16, D), 0)
    for step in range(STEPS):
        shift = mod[pl.ds(start + step, 1), :D]
        gain = 1.0 + mod[pl.ds(start + step, 1), D:]
        folded[step, :64, :] = (weight_centred * gain).astype(BF16)
        is_bias = (extra_row == 0) | (extra_row == 2)
        extra = jnp.where(is_bias, bias_centred * gain, jnp.where(extra_row == 1, shift, 0.0))
        folded[step, 64:80, :] = extra.astype(BF16)
        folded[step, 80:, :] = jnp.zeros((48, D), BF16)

    loads["base"].wait()
    half_lanes = pl.ds(pl.multiple_of(half * half_d, 128), half_d)
    extras = [[None] * 3 for _ in range(STEPS)]
    for member in range(3):
        part = dot(folded[:, :, half_lanes].reshape(STEPS * 128, half_d), base[member, 0])
        for step in range(STEPS):
            piece = part[step * 128:(step + 1) * 128]
            own_part[step, :, member * HD:(member + 1) * HD] = piece
            part_out[step, member * QUERY:(member + 1) * QUERY, :] = piece[:QUERY].astype(BF16)
            extras[step][member] = piece[QUERY:QUERY + 2]
    for step in range(STEPS):
        rest = jnp.concatenate(extras[step] + [jnp.zeros((10, HD), F32)], axis=0)
        part_out[step, 3 * QUERY:, :] = rest.astype(BF16)

    for name in ("latent", "noise0", "out_weight"):
        loads[name].wait()
    hello[half, :own // 2, :] = pack(latent0[...]).astype(BF16)
    hello[half, own // 2:, :] = pack(wout_half[...].astype(F32)).astype(BF16)
    carry[half] = pack(carried(latent0[...], noise0[...], start))
    own_rows = pl.ds(pl.multiple_of(half * own, own), own)
    for step in range(STEPS):
        maps_in[step, :, MAP_ROWS:, :] = jnp.zeros((heads, 128 - MAP_ROWS, 128), BF16)

    def arrived(name):
        arriving.pop(name)()

    def left(name):
        leaving.pop(name)()

    def pair_copy(i, src, dst, device=partner):
        return pltpu.make_async_remote_copy(
            src_ref=src, dst_ref=dst,
            send_sem=pair_send.at[i], recv_sem=pair_recv.at[i],
            device_id=device, device_id_type=MESH,
        )

    def exchange(name, i, out, into, device=partner):
        copy = pair_copy(i, out, out, device)
        copy.start()
        arriving[name] = pair_copy(i, into, into, device).wait_recv
        leaving[name] = copy.wait_send

    hello_copy = pair_copy(0, hello.at[half], hello.at[half])
    carry_copy = pair_copy(1, carry.at[half], carry.at[half])
    part_copies = [pair_copy(3 + step, part_out.at[step], part_in.at[step]) for step in range(STEPS)]

    def start_pair():
        part_copies[0].start()

    def start_late_pair():
        part_copies[1].start()
        carry_copy.start()

    @pl.when(half == 1)
    def _():
        hello_copy.start()

    @pl.when(core == 1)
    def _():
        pl.semaphore_wait(barrier, 1 + in_planes + jnp.where(half == 0, 0, in_columns))
        pl.semaphore_signal(heard, inc=1, device_id=sibling, device_id_type=MESH)

    @pl.when(core == 0)
    def _():
        pl.semaphore_wait(heard, 1)

    @pl.when(half == 1)
    def _():
        each_column(lambda other: column_copy(zlo, other).start())
        start_pair()

    arriving["column"] = lambda: each_column(lambda other: column_copy(other, other).wait_recv())
    leaving["column"] = lambda: each_column(lambda other: column_copy(zlo, other).wait_send())

    def plane_copy(kind, src, dst, peer, slot):
        return pltpu.make_async_remote_copy(
            src_ref=src, dst_ref=dst,
            send_sem=plane_send.at[kind, peer], recv_sem=plane_recv.at[kind, slot],
            device_id=plane(peer), device_id_type=MESH,
        )

    def send_plane(kind, src_of, place_of):
        def receive(offsets=OFFSETS):
            for offset in offsets:
                peer = peer_at(offset)
                plane_copy(kind, src_of(peer), place_of(peer), peer, peer).wait_recv()

        def finish():
            for offset in OFFSETS:
                peer = peer_at(offset)
                plane_copy(kind, src_of(peer), place_of(head), peer, head).wait_send()

        for offset in OFFSETS:
            peer = peer_at(offset)
            plane_copy(kind, src_of(peer), place_of(head), peer, head).start()
        arriving["plane", kind] = receive
        leaving["plane", kind] = finish
        return receive

    stored = zcount * 2 * store_rows
    row = lax.broadcasted_iota(jnp.int32, (stored, 256), 0)
    col = lax.broadcasted_iota(jnp.int32, (stored, 256), 1)
    in_block = col % block_rows
    slot = col // block_rows
    shard = slot % zcount * 2 + slot // zcount
    source = jnp.where(in_block < store_rows, shard * store_rows + in_block, -1)
    place = (row == source).astype(F32).astype(BF16)
    loads["order"].wait()
    order = jnp.broadcast_to((order_ref[...] + 1).astype(F32), (16, stored)).astype(BF16)
    order = dot(order, place)[0:1].astype(jnp.int32) - 1
    total = (pairs + heads) * 16
    line = lax.broadcasted_iota(jnp.int32, (total, 256), 0)
    entry = line & 15
    member_of = entry - 3 * ((entry * 11) >> 5)
    target = jnp.where(entry < 12, member_of * per_member + 2 * (line >> 4), -8)
    perm_even[...] = (target == order).astype(F32).astype(BF16)
    perm_odd[...] = (target + 1 == order).astype(F32).astype(BF16)

    arrived("column")
    exchange("sibling", 2, store.at[core], store.at[1 - core], sibling)

    @pl.when(half == 0)
    def _():
        pl.semaphore_wait(ready, 1)
        hello_copy.start()
        start_pair()

    @pl.when(half == 1)
    def _():
        start_late_pair()

    arrived("sibling")
    blocks = store[...].reshape(256, 256)
    even = dot(perm_even[...], blocks)
    odd = dot(perm_odd[...], blocks)
    lane = lax.broadcasted_iota(jnp.int32, (total, 128), 1)
    entry = lax.broadcasted_iota(jnp.int32, (total, 128), 0) & 15
    rank = (entry * 11) >> 5
    even = jnp.where(rank < 2, even[:, :128], even[:, 128:])
    odd = jnp.where(rank < 2, odd[:, :128], odd[:, 128:])
    first = (rank & 1) == 0
    spread = jnp.where(
        lane < 64,
        jnp.where(first, even, pltpu.roll(even, 64, 1)),
        jnp.where(first, pltpu.roll(odd, 64, 1), odd),
    ).astype(BF16)
    lower = jnp.concatenate([spread[i * 16:(i + 1) * 16] for i in range(pairs)], axis=1)
    inner = [dot(lower, folded[step], NT).astype(BF16) for step in range(STEPS)]
    for other in range(heads):
        rank_out[other, :, 0:128] = inner[0]
        rank_out[other, :, 128:256] = inner[1]
        rank_out[other, :, 256:384] = spread[(pairs + other) * 16:(pairs + other + 1) * 16]
    rank_in[head] = rank_out[head]
    send_plane(0, lambda peer: rank_out.at[peer], lambda slot: rank_in.at[slot])

    for name, i, buffer, copy in (("hello", 0, hello, hello_copy), ("carry", 1, carry, carry_copy)):
        arriving[name] = pair_copy(i, buffer.at[1 - half], buffer.at[1 - half]).wait_recv
        leaving[name] = copy.wait_send
    for step in range(STEPS):
        arriving["part", step] = part_copies[step].wait_recv
        leaving["part", step] = part_copies[step].wait_send

    arrived("hello")
    in_weight_bf = win[...]
    latent_in = jnp.concatenate(
        [unpack(hello[i, :own // 2, :].astype(F32)) for i in range(2)], axis=0
    ).astype(BF16)
    tokens[0, head] = token_features(latent_in, in_weight_bf, in_bias)
    send_plane(1, lambda peer: tokens.at[0, head], lambda slot: tokens.at[0, slot])

    arrived(("plane", 0))
    ranks = rank_in[...].reshape(heads * 16, 384)
    entry = lax.broadcasted_iota(jnp.int32, (heads * 16, HD), 0) & 15
    member_of = entry - 3 * ((entry * 11) >> 5)
    upper = ranks[:, 256:].astype(F32)
    upper = jnp.concatenate(
        [jnp.where(member_of == member, upper, 0.0) for member in range(3)], axis=1
    ).astype(BF16)
    low_rank = dot(ranks[:, :256].astype(F32).T.astype(BF16), upper)
    out_weight = jnp.concatenate(
        [unpack(hello[i, own // 2:, :].astype(F32)) for i in range(2)], axis=0
    )
    got_maps = []

    def make_maps(step):
        arrived(("part", step))
        received = part_in[step].astype(F32)
        rest = received[3 * QUERY:]
        received = jnp.concatenate(
            [
                jnp.concatenate(
                    [
                        received[member * QUERY:(member + 1) * QUERY],
                        rest[2 * member:2 * member + 2],
                        rest[2 * member:2 * member + 1],
                        jnp.zeros((128 - QUERY - 3, HD), F32),
                    ],
                    axis=0,
                )
                for member in range(3)
            ],
            axis=1,
        )
        full = own_part[step] + received + low_rank[step * 128:(step + 1) * 128]
        to_score = HD ** (-0.5) * math.log2(math.e)
        queries, keys = full[:, :HD] * to_score, full[:, HD:2 * HD]
        score_map = exact_dot(queries[:ROWS], keys[:QUERY], NT)
        other_columns = exact_dot(keys[QUERY:ROWS], queries, NT)
        value_map = exact_dot(full[:ROWS, 2 * HD:], out_weight)
        maps_out[step, :ROWS, :] = jnp.concatenate([score_map, value_map], axis=1).astype(BF16)
        maps_out[step, ROWS:, :] = other_columns.astype(BF16)
        maps_in[step, head, :MAP_ROWS, :] = maps_out[step]

    def send_maps(step):
        got_maps.append(
            send_plane(
                2 + step,
                lambda peer: maps_out.at[step],
                lambda slot: maps_in.at[step, slot, pl.ds(0, MAP_ROWS)],
            )
        )

    make_maps(0)
    send_maps(0)

    @pl.when(half == 0)
    def _():
        start_late_pair()

    make_maps(1)
    send_maps(1)

    def first_lanes(features):
        lane = lax.broadcasted_iota(jnp.int32, features.shape, 1)
        return jnp.where(lane < KEY, features, jnp.zeros_like(features))

    def mapped(features, step, slots):
        features = first_lanes(features)
        lane = lax.broadcasted_iota(jnp.int32, features.shape, 1)
        result = []
        for slot in slots:
            maps = maps_in[step, slot]
            columns, others = dot(features, maps), dot(features, maps, NT)
            result.append(jnp.where(lane < QUERY, columns, jnp.where(lane < KEY, 0.0, others)))
        return jnp.concatenate(result, axis=0).astype(BF16)

    def attend(queries, keys, step, slots):
        count = queries.shape[0] // len(slots)
        exponent = jnp.exp2(dot(queries, keys, NT))
        weights = exponent * (1.0 / jnp.sum(exponent, axis=-1, keepdims=True))
        attended = first_lanes(dot(weights.astype(BF16), keys)).astype(BF16)
        sides = jnp.concatenate(
            [attended[i * count:(i + 1) * count] for i in range(len(slots))], axis=1
        )
        return dot(sides, jnp.concatenate([maps_in[step, slot] for slot in slots], axis=0))

    near_first = ((0, 0),) + OFFSETS[::-1]

    arrived(("plane", 1))
    keys = tokens[0].reshape(heads * both, 128)
    features = tokens[0, head]
    arriving.pop(("plane", 2))
    velocity = jnp.zeros((both, 128), F32)
    for i in range(0, heads, 4):
        offsets = near_first[i:i + 4]
        got_maps[0](offsets[1:] if i == 0 else offsets)
        slots = [peer_at(offset) for offset in offsets]
        velocity += attend(mapped(features, 0, slots), keys, 0, slots)
    arrived("carry")
    carry_rows = jnp.concatenate([unpack(carry[i]) for i in range(2)], axis=0)
    state[...] = carry_rows + added(velocity[:, C:], start)
    tokens[1, head] = token_features(state[...].astype(BF16), in_weight_bf, in_bias)
    send_plane(4, lambda peer: tokens.at[1, head], lambda slot: tokens.at[1, slot])
    arrived(("plane", 3))
    slots = [peer_at(offset) for offset in near_first]
    queries = mapped(tokens[1, head, own_rows, :], 1, slots)
    arrived(("plane", 4))

    keys = tokens[1].reshape(heads * both, 128)
    velocity = jnp.zeros((own, 128), F32)
    for i in range(0, heads, 8):
        velocity += attend(queries[i * own:(i + 8) * own], keys, 1, slots[i:i + 8])
    velocity = velocity[:, C:]
    loads["noise1"].wait()
    latent = carried(state[own_rows, :], noise1[...], start + 1) + added(velocity, start + 1)
    result[0] = jnp.concatenate([latent, velocity], axis=1)

    for name in list(leaving):
        left(name)


def shards(groups, heads):
    def run(
        latent, step_noise, start_index, mod_table, in_weight, in_bias,
        base_weight, factor_store, block_order, out_weight,
    ):
        own = latent.shape[1]
        block_rows = (factor_store.shape[0] + 15) // 16 * 16
        total = (D // 128 + heads) * 16
        vmem = pl.BlockSpec(memory_space=pltpu.VMEM)
        anywhere = pl.BlockSpec(memory_space=pl.ANY)
        result = pl.pallas_call(
            functools.partial(kernel, groups, heads),
            out_shape=jax.ShapeDtypeStruct((1, own, 2 * C), F32),
            in_specs=[
                pl.BlockSpec(memory_space=pltpu.SMEM),
                *[anywhere] * 9,
            ],
            out_specs=vmem,
            scratch_shapes=[
                pltpu.VMEM(mod_table.shape, F32),
                pltpu.VMEM(in_weight.shape, BF16),
                pltpu.VMEM((1, D), F32),
                pltpu.VMEM(base_weight.shape, BF16),
                pltpu.VMEM(factor_store.shape, BF16),
                pltpu.VMEM((1, block_order.shape[0]), jnp.int32),
                pltpu.VMEM((own, C), F32),
                pltpu.VMEM((own, C), F32),
                pltpu.VMEM((own, C), F32),
                pltpu.VMEM(out_weight.shape, BF16),
                pltpu.VMEM((2, own // 2 + 32, 128), BF16),
                pltpu.VMEM((2, own // 2, 128), F32),
                pltpu.VMEM((2 * own, C), F32),
                pltpu.VMEM((2, groups // 2, block_rows, 256), BF16),
                pltpu.VMEM((total, 256), BF16),
                pltpu.VMEM((total, 256), BF16),
                pltpu.VMEM((STEPS, 128, D), BF16),
                pltpu.VMEM((STEPS, 128, 3 * HD), F32),
                pltpu.VMEM((STEPS, 3 * QUERY + 16, HD), BF16),
                pltpu.VMEM((STEPS, 3 * QUERY + 16, HD), BF16),
                pltpu.VMEM((heads, 16, 384), BF16),
                pltpu.VMEM((heads, 16, 384), BF16),
                pltpu.VMEM((STEPS, heads, 2 * own, 128), BF16),
                pltpu.VMEM((STEPS, MAP_ROWS, 128), BF16),
                pltpu.VMEM((STEPS, heads, 128, 128), BF16),
                pltpu.SemaphoreType.DMA((10,)),
                pltpu.SemaphoreType.DMA((groups // 2,)),
                pltpu.SemaphoreType.DMA((groups // 2,)),
                pltpu.SemaphoreType.DMA((5,)),
                pltpu.SemaphoreType.DMA((5,)),
                pltpu.SemaphoreType.DMA((5, heads)),
                pltpu.SemaphoreType.DMA((5, heads)),
                pltpu.SemaphoreType.REGULAR,
                pltpu.SemaphoreType.REGULAR,
            ],
            compiler_params=pltpu.CompilerParams(
                collective_id=0, has_side_effects=True, vmem_limit_bytes=63 * 1024 * 1024
            ),
        )(
            start_index, latent, step_noise, mod_table, in_weight, in_bias.reshape(1, -1),
            base_weight, factor_store, block_order.reshape(1, -1), out_weight,
        )
        return result[:, :, :C], result[:, :, C:]

    return run


def solution(mesh):
    in_specs = (
        P("grp", "seq", None),
        P("grp", None, "seq", None),
        P("grp"),
        P(),
        P(),
        P(),
        P(None, "seq", None, None),
        P("grp", None),
        P(),
        P("seq", None),
    )
    out_specs = (P("grp", "seq", None), P("grp", "seq", None))
    run = shards(mesh.shape["grp"], mesh.shape["seq"] // 2)
    return jax.shard_map(run, mesh=mesh, in_specs=in_specs, out_specs=out_specs, check_vma=False)
```
